32 devices in a mesh: runs: 2 (over y), sec: 4 (over z), mpo: 2 (over x), rep: 2 (over core).
Axes of the slice: x: 2, y: 2, z: 4, core: 2. Of those that a mesh axis runs over, the one named last changes fastest.
Arguments:
- wavefunction: bfloat16 [128, 256, 256], P(('runs', 'sec'), None, 'rep'), parts along dimension 0, may hold values from -6 to 6
- left_env: bfloat16 [16, 10, 256, 256], P(('runs', 'sec'), 'mpo'), parts along dimension 0, may hold values from -0.375 to 0.375
- right_env: bfloat16 [16, 10, 256, 256], P(('runs', 'sec'), 'mpo', None, 'rep'), parts along dimension 0, may hold values from -0.125 to 0.125
- send_order: int32 [4, 16], P('sec'), may hold values from 0 to 15, each once within a row
- recv_order: int32 [4, 16], P('sec'), may hold values from 0 to 15, each once within a row
- pair_left: int32 [4, 16], P('sec'), may hold values from 0 to 1
- pair_right: int32 [4, 16], P('sec'), may hold values from 0 to 1
- left_size: int32 [8], P('sec'), may hold values from 128 to 256
- right_size: int32 [8], P('sec'), may hold values from 128 to 256
- mpo_pattern: int32 [8, 10], P('sec', 'mpo'), may hold values 0 or 1
Outputs:
- applied: bfloat16 [128, 256, 256], P(('runs', 'sec'), 'mpo', 'rep'), parts along dimension 0
The draws below stay inside these ranges and needn't reach their ends.
There are 2 independent parts, one for each index of `runs`. The reference program is written for one: setup_inputs(seed, part) draws one part's arguments, and reference() takes and returns one part's arrays. A program takes and returns all parts, laid end to end along the dimension named above; an argument that names none is the same for every part. Nothing has to cross between parts.
Inputs may be any that keep to these rules, and one draw needn't show every extreme that they name: `send_order`: each row names each of 0 to 15 once. `recv_order`: each row names each of 0 to 15 once.
All inputs are finite; a program needn't handle non-finite values. No bound on the sum of `mpo_pattern` on one device may be relied on, other than what follows from the above.
Results may differ from the reference program's by a relative error of at most 0.0051.
Values may be sent and summed in bfloat16 or wider, within the bound.
A program may use at most 128 MiB of HBM per device.

```python
import jax
import jax.numpy as jnp
from jax import lax

S = 256
PD = 16
LS = 2
RS = 2
W = 10
BLOCKS = 64
LEFTS = 8
RIGHTS = 8
N_SEC = 4


def place_ends(array, key, smallest, high):
    longest = array.shape.index(max(array.shape))
    spots = []
    for shift in (0, 1):
        where = [jax.random.randint(jax.random.fold_in(key, axis), (), 0, length) for axis, length in enumerate(array.shape)]
        where[longest] = (where[longest] + shift) % array.shape[longest]
        spots.append(tuple(where))
    return array.at[spots[0]].set(smallest).at[spots[1]].set(high)


def shard_levels(stream_key, shape, split, low, top_value):
    gain, own = 1.0, jax.random.fold_in(stream_key, 6)
    for position, blocks in split:
        steps = jnp.exp(jax.random.uniform(jax.random.fold_in(own, position), (blocks,), jnp.float32, low / len(split), top_value / len(split)))
        gain = gain * jnp.repeat(steps, shape[position] // blocks).reshape([-1 if axis == position else 1 for axis in range(len(shape))])
    return gain


def bell_draw(stream_key, dims, width, most, split=(), held_as=jnp.bfloat16):
    values = width * jax.random.normal(stream_key, dims, jnp.float32)
    if split:
        values = values * shard_levels(stream_key, dims, split, -0.22, 0.18)
    return jnp.clip(values, -most, most).astype(held_as)


def setup_inputs(seed: int = 0, part: int = 0) -> dict:
    arg_keys = jax.random.split(jax.random.key(seed), 11)
    part_keys = jax.random.split(jax.random.fold_in(arg_keys[10], part), 11)
    wavefunction = bell_draw(part_keys[0], (BLOCKS, S, S), 1.0, 6.0, ((0, 4), (2, 2)))
    left_env = bell_draw(part_keys[1], (LEFTS, W, S, S), S ** -0.5, 0.375, ((0, 4), (1, 2)))
    right_env = bell_draw(part_keys[2], (RIGHTS, W, S, S), (S * W) ** -0.5, 0.125, ((0, 4), (1, 2), (3, 2)))
    send_order = jax.vmap(lambda own: jax.random.permutation(own, PD))(jax.random.split(arg_keys[3], N_SEC)).reshape((N_SEC, PD)).astype(jnp.int32)
    recv_order = jax.vmap(lambda own: jax.random.permutation(own, PD))(jax.random.split(arg_keys[4], N_SEC)).reshape((N_SEC, PD)).astype(jnp.int32)
    pair_left = place_ends(jax.random.randint(arg_keys[5], (N_SEC, PD), 0, LS), jax.random.fold_in(arg_keys[5], 1), 0, LS - 1).astype(jnp.int32)
    pair_right = place_ends(jax.random.randint(arg_keys[6], (N_SEC, PD), 0, RS), jax.random.fold_in(arg_keys[6], 1), 0, RS - 1).astype(jnp.int32)
    left_size = place_ends(jax.random.randint(arg_keys[7], (LEFTS,), S // 2, S + 1), jax.random.fold_in(arg_keys[7], 1), S // 2, S).astype(jnp.int32)
    right_size = place_ends(jax.random.randint(arg_keys[8], (RIGHTS,), S // 2, S + 1), jax.random.fold_in(arg_keys[8], 1), S // 2, S).astype(jnp.int32)
    mpo_pattern = place_ends((jax.random.randint(arg_keys[9], (LEFTS, W), 0, 4) < 3).astype(jnp.int32), jax.random.fold_in(arg_keys[9], 1), 0, 1)
    return {"wavefunction": wavefunction, "left_env": left_env, "right_env": right_env, "send_order": send_order, "recv_order": recv_order, "pair_left": pair_left, "pair_right": pair_right, "left_size": left_size, "right_size": right_size, "mpo_pattern": mpo_pattern}


def reference(wavefunction, left_env, right_env, send_order, recv_order, pair_left, pair_right, left_size, right_size, mpo_pattern):
    per_peer = PD // N_SEC
    row_index = jnp.arange(S, dtype=jnp.int32)

    def output_block(flat_id):
        target = flat_id // PD
        out_slot = flat_id % PD
        arrival = recv_order[target, out_slot]
        source = arrival // per_peer
        sent_slot = target * per_peer + arrival % per_peer
        local_pair = send_order[source, sent_slot]
        pair_id = source * PD + local_pair
        left_id = source * LS + pair_left[source, local_pair]
        right_id = target * RS + pair_right[target, out_slot]
        keep_left = (row_index < left_size[left_id]).astype(jnp.float32)
        keep_right = (row_index < right_size[right_id]).astype(jnp.float32)
        masked = (wavefunction[pair_id].astype(jnp.float32) * keep_left[:, None]).astype(jnp.bfloat16)
        left_blocks = left_env[left_id].astype(jnp.float32)
        interim = jnp.einsum('wik,kj->wij', left_blocks, masked.astype(jnp.float32))
        weights = mpo_pattern[left_id].astype(jnp.float32)
        interim = (interim * keep_left[None, :, None] * weights[:, None, None]).astype(jnp.bfloat16)
        right_mask = keep_right[:, None] * keep_right[None, :]
        right_blocks = (right_env[right_id].astype(jnp.float32) * right_mask[None, :, :]).astype(jnp.bfloat16)
        result = jnp.einsum('wik,wkj->ij', interim.astype(jnp.float32), right_blocks.astype(jnp.float32))
        return result.astype(jnp.bfloat16)

    return lax.map(output_block, jnp.arange(N_SEC * PD, dtype=jnp.int32))
```

```python
import jax
import jax.numpy as jnp
from jax import lax
from jax.sharding import PartitionSpec as P

BF = jnp.bfloat16
F32 = jnp.float32


def local(
    wavefunction,
    left_env,
    right_env,
    send_order,
    recv_order,
    pair_left,
    pair_right,
    left_size,
    right_size,
    mpo_pattern,
):
    width = wavefunction.shape[1]
    half = wavefunction.shape[2]
    pairs = wavefunction.shape[0]
    peers = lax.axis_size("sec")
    reps = lax.axis_size("rep")
    mpos = lax.axis_size("mpo")
    lefts, nw = left_env.shape[:2]
    send_rows = send_order[0]
    rows = jnp.arange(width, dtype=jnp.int32)
    left_ids = pair_left[0][send_rows]
    keep = (rows[None, :] < left_size[left_ids][:, None]).astype(BF)
    source = wavefunction[send_rows] * keep[:, :, None]
    tag = jnp.broadcast_to(left_ids.astype(BF)[:, None, None], (pairs, 16, half))
    source = jnp.concatenate([source, tag], axis=1)
    arrived = lax.all_to_all(source, "sec", split_axis=0, concat_axis=0, tiled=True)
    arrived = arrived[recv_order[0]]
    own = arrived[:, width, 0].astype(jnp.int32)
    left_of = own + (recv_order[0] // (pairs // peers)) * lefts
    arrived = lax.all_gather(arrived[:, :width], "rep", axis=2, tiled=True)

    keep_l = (rows[None, :] < left_size[:, None]).astype(BF)
    scale = keep_l[:, None, :, None] * mpo_pattern.astype(BF)[:, :, None, None]
    masked_left = left_env * scale
    part = width // reps
    mine = lax.dynamic_slice_in_dim(masked_left, lax.axis_index("rep") * part, part, axis=2)
    full = lax.all_gather(mine, "sec", axis=0, tiled=True)
    full = lax.all_gather(full, "rep", axis=2, tiled=True)
    blocks = full[left_of]
    interim = jnp.einsum("pwik,pkj->pwij", blocks, arrived, preferred_element_type=F32).astype(BF)

    right_ids = pair_right[0]
    keep_r = rows[None, :] < right_size[:, None]
    cols = jnp.arange(half, dtype=jnp.int32) + lax.axis_index("rep") * half
    keep_c = cols[None, :] < right_size[:, None]
    mask = (keep_r[:, :, None] & keep_c[:, None, :]).astype(BF)
    right_blocks = (right_env * mask[:, None])[right_ids]
    value = jnp.einsum("pwik,pwkj->pij", interim, right_blocks, preferred_element_type=F32)
    value = value.astype(BF).reshape(pairs, mpos, width // mpos, half)
    value = lax.all_to_all(value, "mpo", split_axis=1, concat_axis=1, tiled=True)
    return jnp.sum(value.astype(F32), axis=1).astype(BF)


def solution(mesh):
    placed = (
        P(("runs", "sec"), None, "rep"),
        P(("runs", "sec"), "mpo", None, None),
        P(("runs", "sec"), "mpo", None, "rep"),
        P("sec", None),
        P("sec", None),
        P("sec", None),
        P("sec", None),
        P("sec"),
        P("sec"),
        P("sec", "mpo"),
    )
    return jax.shard_map(
        local,
        mesh=mesh,
        in_specs=placed,
        out_specs=P(("runs", "sec"), "mpo", "rep"),
        check_vma=False,
    )
```

```python
import functools

import jax
import jax.numpy as jnp
from jax import lax
from jax.experimental import pallas as pl
from jax.experimental.pallas import tpu as pltpu
from jax.sharding import PartitionSpec as P

BF = jnp.bfloat16
F32 = jnp.float32
MESH = pl.DeviceIdType.MESH


def kernel(
    n,
    mpos,
    send_ref,
    recv_ref,
    pair_ref,
    right_of_ref,
    lsize_ref,
    rsize_ref,
    pattern_ref,
    wf_ref,
    left_ref,
    right_ref,
    out_ref,
    lbuf,
    rbuf,
    stage,
    tagstage,
    wbuf,
    tagbuf,
    total,
    rounded,
    mbuf,
    ls_own,
    ls,
    lr,
    cs,
    cr,
    ws,
    wr,
    vs,
    vr,
    ts,
    tr,
    ms,
    mr,
):
    me = lax.axis_index("sec")
    m = lax.axis_index("mpo")
    c = lax.axis_index("rep")
    other = 1 - c
    lefts, nw, width = left_ref.shape[:3]
    rights = right_ref.shape[0]
    half = wf_ref.shape[2]
    per = wf_ref.shape[0] // n
    part = width // 2
    mrows = width // mpos

    barrier = pltpu.get_barrier_semaphore()
    for t in range(1, n):
        pl.semaphore_signal(
            barrier, inc=1, device_id={"sec": lax.rem(me + t, n)}, device_id_type=MESH
        )
    for t in range(1, mpos):
        pl.semaphore_signal(
            barrier, inc=1, device_id={"mpo": lax.rem(m + t, mpos)}, device_id_type=MESH
        )
    pl.semaphore_signal(barrier, inc=1, device_id={"rep": other}, device_id_type=MESH)

    row = lax.broadcasted_iota(jnp.int32, (width, width), 0)
    hrow = lax.broadcasted_iota(jnp.int32, (width, half), 0)
    hcol = lax.broadcasted_iota(jnp.int32, (width, half), 1) + c * half

    def my_rows(d, l):
        return lbuf.at[d, l, :, pl.ds(pl.multiple_of(c * part, part), part), :]

    def hop(d, l, step, sem):
        return pltpu.make_async_remote_copy(
            src_ref=my_rows(d, l),
            dst_ref=my_rows(d, l),
            send_sem=sem,
            recv_sem=lr.at[d, l],
            device_id={"sec": me + step},
            device_id_type=MESH,
        )

    def cross(d, l):
        return pltpu.make_async_remote_copy(
            src_ref=my_rows(d, l),
            dst_ref=my_rows(d, l),
            send_sem=cs.at[d, l],
            recv_sem=cr.at[d, l],
            device_id={"rep": other},
            device_id_type=MESH,
        )

    def wave(e):
        return pltpu.make_async_remote_copy(
            src_ref=stage.at[e],
            dst_ref=wbuf.at[me, c],
            send_sem=ws.at[e],
            recv_sem=wr.at[me],
            device_id={"sec": e},
            device_id_type=MESH,
        )

    def wave_from(d):
        return pltpu.make_async_remote_copy(
            src_ref=stage.at[d],
            dst_ref=wbuf.at[d, c],
            send_sem=ws.at[d],
            recv_sem=wr.at[d],
            device_id={"sec": d},
            device_id_type=MESH,
        )

    def wave_cross(d, side):
        return pltpu.make_async_remote_copy(
            src_ref=wbuf.at[d, side],
            dst_ref=wbuf.at[d, side],
            send_sem=vs.at[d],
            recv_sem=vr.at[d],
            device_id={"rep": other},
            device_id_type=MESH,
        )

    def tags(e, slot):
        return pltpu.make_async_remote_copy(
            src_ref=tagstage.at[e],
            dst_ref=tagbuf.at[slot],
            send_sem=ts.at[e],
            recv_sem=tr.at[slot],
            device_id={"sec": e},
            device_id_type=MESH,
        )

    def partial_to(d, o):
        target = lax.rem(m + o, mpos)
        rows = pl.ds(pl.multiple_of(target * mrows, mrows), mrows)
        return pltpu.make_async_remote_copy(
            src_ref=rounded.at[d, :, rows, :],
            dst_ref=mbuf.at[o - 1, d],
            send_sem=ms.at[d, o - 1],
            recv_sem=mr.at[d, o - 1],
            device_id={"mpo": target},
            device_id_type=MESH,
        )

    for l in range(lefts):
        size = lsize_ref[l]
        keep = jnp.where(row < size, 1.0, 0.0)
        for w in range(nw):
            scale = (keep * pattern_ref[l, w].astype(F32)).astype(BF)
            lbuf[me, l, w] = left_ref[l, w] * scale
        if l == 0:
            pl.semaphore_wait(barrier, n + mpos - 1)

        @pl.when(me + 1 < n)
        def _():
            hop(me, l, 1, ls_own.at[0, l]).start()

        @pl.when(me > 0)
        def _():
            hop(me, l, -1, ls_own.at[1, l]).start()

    def fill(e, carry):
        for k in range(per):
            block = send_ref[0, e * per + k]
            left = pair_ref[0, block]
            keep = jnp.where(hrow < lsize_ref[left], 1.0, 0.0).astype(BF)
            stage[e, k] = wf_ref[block] * keep
            for l in range(lefts):
                flag = jnp.where(left == l, 1.0, 0.0)
                tagstage[e, k, l] = jnp.full((16, 128), flag, F32).astype(BF)

        @pl.when(e != me)
        def _():
            tags(e, me).start()
            wave(e).start()

        return carry

    lax.fori_loop(0, n, fill, 0)
    wbuf[me, c] = stage[me]
    tagbuf[me] = tagstage[me]
    wave_cross(me, c).start()

    for b in range(rights):
        size = rsize_ref[b]
        keep = jnp.where(jnp.logical_and(hrow < size, hcol < size), 1.0, 0.0).astype(BF)
        for w in range(nw):
            rbuf[b, w] = right_ref[b, w] * keep

    def compute(d):
        def one(k, carry):
            x = jnp.concatenate([wbuf[d, 0, k], wbuf[d, 1, k]], axis=1)
            b = right_of_ref[0, d * per + k]
            flags = []
            for l in range(lefts):
                flag = tagbuf[d, k, l]
                flag = jnp.concatenate([flag] * (width // 128), axis=1)
                flags.append(jnp.concatenate([flag] * (width // 16), axis=0))
            acc = jnp.zeros((width, half), F32)
            for w in range(nw):
                env = lbuf[d, 0, w] * flags[0]
                for l in range(1, lefts):
                    env = env + lbuf[d, l, w] * flags[l]
                y = jnp.dot(env, x, preferred_element_type=F32).astype(BF)
                acc = acc + jnp.dot(y, rbuf[b, w], preferred_element_type=F32)
            total[d, k] = acc
            rounded[d, k] = acc.astype(BF)
            return carry

        lax.fori_loop(0, per, one, 0)
        for o in range(1, mpos):
            partial_to(d, o).start()

    wave_cross(me, other).wait_recv()
    compute(me)

    def arrive(t, carry):
        for l in range(lefts):
            for step in (1, -1):
                d = me - step * t

                @pl.when(jnp.logical_and(d >= 0, d < n))
                def _():
                    if l == 0:
                        tags(d, d).wait_recv()
                        wave_from(d).wait_recv()
                        wave_cross(d, c).start()
                    hop(d, l, -step, ls.at[d, l]).wait_recv()
                    nxt = me + step

                    @pl.when(jnp.logical_and(nxt >= 0, nxt < n))
                    def _():
                        hop(d, l, step, ls.at[d, l]).start()

                    cross(d, l).start()

        return carry

    def finish(t):
        for step in (1, -1):
            d = me - step * t

            @pl.when(jnp.logical_and(d >= 0, d < n))
            def _():
                wave_cross(d, other).wait_recv()
                for l in range(lefts):
                    cross(d, l).wait_recv()
                compute(d)

    def turn(t, carry):
        arrive(t, 0)

        @pl.when(t > 1)
        def _():
            finish(t - 1)

        return carry

    lax.fori_loop(1, n, turn, 0)
    finish(n - 1)

    for l in range(lefts):

        @pl.when(me + 1 < n)
        def _():
            hop(me, l, 1, ls_own.at[0, l]).wait_send()

        @pl.when(me > 0)
        def _():
            hop(me, l, -1, ls_own.at[1, l]).wait_send()

    def drain(d, carry):
        wave_cross(d, c).wait_send()
        for o in range(1, mpos):
            partial_to(d, o).wait()

        @pl.when(d != me)
        def _():
            wave(d).wait_send()
            tags(d, me).wait_send()
            for l in range(lefts):
                cross(d, l).wait_send()

        @pl.when(jnp.logical_and(d < me, me + 1 < n))
        def _():
            for l in range(lefts):
                hop(d, l, 1, ls.at[d, l]).wait_send()

        @pl.when(jnp.logical_and(d > me, me > 0))
        def _():
            for l in range(lefts):
                hop(d, l, -1, ls.at[d, l]).wait_send()

        return carry

    lax.fori_loop(0, n, drain, 0)

    own = pl.ds(pl.multiple_of(m * mrows, mrows), mrows)

    def emit(i, carry):
        r = recv_ref[0, i]
        d, k = r // per, lax.rem(r, per)
        value = total[d, k, own, :]
        for o in range(1, mpos):
            value = value + mbuf[o - 1, d, k].astype(F32)
        out_ref[i] = value.astype(BF)
        return carry

    lax.fori_loop(0, n * per, emit, 0)


def local(
    n,
    mpos,
    wavefunction,
    left_env,
    right_env,
    send_order,
    recv_order,
    pair_left,
    pair_right,
    left_size,
    right_size,
    mpo_pattern,
):
    pairs, width, half = wavefunction.shape
    per = pairs // n
    lefts, nw = left_env.shape[:2]
    slots = jnp.arange(pairs, dtype=jnp.int32)
    match = recv_order[0][None, :] == slots[:, None]
    right_of = jnp.sum(jnp.where(match, pair_right[0][None, :], 0), axis=1)[None, :]
    smem = pl.BlockSpec(memory_space=pltpu.SMEM)
    vmem = pl.BlockSpec(memory_space=pltpu.VMEM)
    dma = pltpu.SemaphoreType.DMA
    others = max(mpos - 1, 1)
    return pl.pallas_call(
        functools.partial(kernel, n, mpos),
        out_shape=jax.ShapeDtypeStruct((pairs, width // mpos, half), BF),
        in_specs=[smem] * 7 + [vmem] * 3,
        out_specs=vmem,
        scratch_shapes=[
            pltpu.VMEM((n, lefts, nw, width, width), BF),
            pltpu.VMEM(right_env.shape, BF),
            pltpu.VMEM((n, per, width, half), BF),
            pltpu.VMEM((n, per, lefts, 16, 128), BF),
            pltpu.VMEM((n, 2, per, width, half), BF),
            pltpu.VMEM((n, per, lefts, 16, 128), BF),
            pltpu.VMEM((n, per, width, half), F32),
            pltpu.VMEM((n, per, width, half), BF),
            pltpu.VMEM((others, n, per, width // mpos, half), BF),
            dma((2, lefts)),
            dma((n, lefts)),
            dma((n, lefts)),
            dma((n, lefts)),
            dma((n, lefts)),
            dma((n,)),
            dma((n,)),
            dma((n,)),
            dma((n,)),
            dma((n,)),
            dma((n,)),
            dma((n, others)),
            dma((n, others)),
        ],
        compiler_params=pltpu.CompilerParams(
            collective_id=0, has_side_effects=True, vmem_limit_bytes=52 * 1024 * 1024
        ),
        cost_estimate=pl.CostEstimate(
            flops=6 * pairs * nw * width * width * half,
            bytes_accessed=8 * pairs * width * half,
            transcendentals=0,
        ),
        name="apply_blocks",
    )(
        send_order,
        recv_order,
        pair_left,
        right_of,
        left_size,
        right_size,
        mpo_pattern,
        wavefunction,
        left_env,
        right_env,
    )


def solution(mesh):
    placed = (
        P(("runs", "sec"), None, "rep"),
        P(("runs", "sec"), "mpo", None, None),
        P(("runs", "sec"), "mpo", None, "rep"),
        P("sec", None),
        P("sec", None),
        P("sec", None),
        P("sec", None),
        P("sec"),
        P("sec"),
        P("sec", "mpo"),
    )
    return jax.shard_map(
        functools.partial(local, mesh.shape["sec"], mesh.shape["mpo"]),
        mesh=mesh,
        in_specs=placed,
        out_specs=P(("runs", "sec"), "mpo", "rep"),
        check_vma=False,
    )
```

```python
import functools

import jax
import jax.numpy as jnp
from jax import lax
from jax.experimental import pallas as pl
from jax.experimental.pallas import tpu as pltpu
from jax.sharding import PartitionSpec as P

BF = jnp.bfloat16
F32 = jnp.float32
MESH = pl.DeviceIdType.MESH


def kernel(
    n,
    mpos,
    send_ref,
    recv_ref,
    pair_ref,
    right_of_ref,
    lsize_ref,
    rsize_ref,
    pattern_ref,
    wf_hbm,
    left_hbm,
    right_hbm,
    out_ref,
    wf_ref,
    left_ref,
    right_ref,
    load,
    lbuf,
    rbuf,
    stage,
    tagstage,
    wbuf,
    tagbuf,
    total,
    rounded,
    mbuf,
    ls_own,
    ls,
    lr,
    cs,
    cr,
    ws,
    wr,
    xs,
    xr,
    vs,
    vr,
    ts,
    tr,
    ms,
    mr,
):
    me = lax.axis_index("sec")
    m = lax.axis_index("mpo")
    c = lax.axis_index("rep")
    other = 1 - c
    lefts, nw, width = left_ref.shape[:3]
    rights = right_ref.shape[0]
    half = wf_ref.shape[2]
    per = wf_ref.shape[0] // n
    part = width // 2
    mrows = width // mpos

    load_left = pltpu.make_async_copy(left_hbm, left_ref, load.at[0])
    load_wf = pltpu.make_async_copy(wf_hbm, wf_ref, load.at[1])
    load_right = pltpu.make_async_copy(right_hbm, right_ref, load.at[2])
    load_left.start()
    load_wf.start()
    load_right.start()
    barrier = pltpu.get_barrier_semaphore()
    for t in range(1, n):
        pl.semaphore_signal(
            barrier, inc=1, device_id={"sec": lax.rem(me + t, n)}, device_id_type=MESH
        )
    for t in range(1, mpos):
        pl.semaphore_signal(
            barrier, inc=1, device_id={"mpo": lax.rem(m + t, mpos)}, device_id_type=MESH
        )
    pl.semaphore_signal(barrier, inc=1, device_id={"rep": other}, device_id_type=MESH)

    row = lax.broadcasted_iota(jnp.int32, (width, width), 0)
    hrow = lax.broadcasted_iota(jnp.int32, (width, half), 0)
    hcol = lax.broadcasted_iota(jnp.int32, (width, half), 1) + c * half

    def my_rows(d, q):
        return lbuf.at[d, q, :, pl.ds(pl.multiple_of(c * part, part), part), :]

    def hop(d, q, step, sem):
        return pltpu.make_async_remote_copy(
            src_ref=my_rows(d, q),
            dst_ref=my_rows(d, q),
            send_sem=sem,
            recv_sem=lr.at[d, q],
            device_id={"sec": me + step},
            device_id_type=MESH,
        )

    def cross(d, q):
        return pltpu.make_async_remote_copy(
            src_ref=my_rows(d, q),
            dst_ref=my_rows(d, q),
            send_sem=cs.at[d, q],
            recv_sem=cr.at[d, q],
            device_id={"rep": other},
            device_id_type=MESH,
        )

    own = pl.ds(pl.multiple_of(m * mrows, mrows), mrows)

    def wave(e, slot):
        return pltpu.make_async_remote_copy(
            src_ref=stage.at[e, :, own, :],
            dst_ref=wbuf.at[slot, c, :, own, :],
            send_sem=ws.at[e],
            recv_sem=wr.at[slot],
            device_id={"sec": e},
            device_id_type=MESH,
        )

    def wave_share(d, o):
        return pltpu.make_async_remote_copy(
            src_ref=wbuf.at[d, c, :, own, :],
            dst_ref=wbuf.at[d, c, :, own, :],
            send_sem=xs.at[d, o - 1],
            recv_sem=xr.at[d, o - 1],
            device_id={"mpo": lax.rem(m + o, mpos)},
            device_id_type=MESH,
        )

    def wave_shared(d, o):
        source = lax.rem(m + mpos - o, mpos)
        rows = pl.ds(pl.multiple_of(source * mrows, mrows), mrows)
        return pltpu.make_async_remote_copy(
            src_ref=wbuf.at[d, c, :, rows, :],
            dst_ref=wbuf.at[d, c, :, rows, :],
            send_sem=xs.at[d, o - 1],
            recv_sem=xr.at[d, o - 1],
            device_id={"mpo": source},
            device_id_type=MESH,
        )

    def wave_cross(d, side):
        return pltpu.make_async_remote_copy(
            src_ref=wbuf.at[d, side],
            dst_ref=wbuf.at[d, side],
            send_sem=vs.at[d],
            recv_sem=vr.at[d],
            device_id={"rep": other},
            device_id_type=MESH,
        )

    def tags(e, slot):
        return pltpu.make_async_remote_copy(
            src_ref=tagstage.at[e],
            dst_ref=tagbuf.at[slot],
            send_sem=ts.at[e],
            recv_sem=tr.at[slot],
            device_id={"sec": e},
            device_id_type=MESH,
        )

    def partial_to(d, o):
        target = lax.rem(m + o, mpos)
        rows = pl.ds(pl.multiple_of(target * mrows, mrows), mrows)
        return pltpu.make_async_remote_copy(
            src_ref=rounded.at[d, :, rows, :],
            dst_ref=mbuf.at[o - 1, d],
            send_sem=ms.at[d, o - 1],
            recv_sem=mr.at[d, o - 1],
            device_id={"mpo": target},
            device_id_type=MESH,
        )

    keeps = [jnp.where(row < lsize_ref[l], 1.0, 0.0) for l in range(lefts)]
    load_left.wait()
    for q in range(nw):
        for l in range(lefts):
            scale = (keeps[l] * pattern_ref[l, q].astype(F32)).astype(BF)
            lbuf[me, q, l] = left_ref[l, q] * scale
        if q == 0:
            pl.semaphore_wait(barrier, n + mpos - 1)

        @pl.when(me + 1 < n)
        def _():
            hop(me, q, 1, ls_own.at[0, q]).start()

        @pl.when(me > 0)
        def _():
            hop(me, q, -1, ls_own.at[1, q]).start()

    load_wf.wait()

    def fill(e, carry):
        for k in range(per):
            block = send_ref[0, e * per + k]
            left = pair_ref[0, block]
            keep = jnp.where(hrow < lsize_ref[left], 1.0, 0.0).astype(BF)
            stage[e, k] = wf_ref[block] * keep
            for l in range(lefts):
                flag = jnp.where(left == l, 1.0, 0.0)
                tagstage[e, k, l] = jnp.full((16, 128), flag, F32).astype(BF)

        @pl.when(e != me)
        def _():
            tags(e, me).start()
            wave(e, me).start()

        return carry

    lax.fori_loop(0, n, fill, 0)
    wbuf[me, c] = stage[me]
    tagbuf[me] = tagstage[me]
    wave_cross(me, c).start()

    load_right.wait()
    for b in range(rights):
        size = rsize_ref[b]
        keep = jnp.where(jnp.logical_and(hrow < size, hcol < size), 1.0, 0.0).astype(BF)
        for w in range(nw):
            rbuf[b, w] = right_ref[b, w] * keep

    def compute(d, q):
        for k in range(per):
            x = jnp.concatenate([wbuf[d, 0, k], wbuf[d, 1, k]], axis=1)
            b = right_of_ref[0, d * per + k]
            env = None
            for l in range(lefts):
                flag = tagbuf[d, k, l]
                flag = jnp.concatenate([flag] * (width // 128), axis=1)
                flag = jnp.concatenate([flag] * (width // 16), axis=0)
                term = lbuf[d, q, l] * flag
                env = term if env is None else env + term
            y = jnp.dot(env, x, preferred_element_type=F32).astype(BF)
            total[d, k] += jnp.dot(y, rbuf[b, q], preferred_element_type=F32)

        @pl.when(q == nw - 1)
        def _():
            for k in range(per):
                rounded[d, k] = total[d, k].astype(BF)
            for o in range(1, mpos):
                partial_to(d, o).start()

    def clear(d, carry):
        for k in range(per):
            total[d, k] = jnp.zeros((width, half), F32)
        return carry

    lax.fori_loop(0, n, clear, 0)

    wave_cross(me, other).wait_recv()

    def first(q, carry):
        compute(me, q)
        return carry

    lax.fori_loop(0, nw, first, 0)

    def arrive(t, q):
        for step in (1, -1):
            d = me - step * t

            @pl.when(jnp.logical_and(d >= 0, d < n))
            def _():
                hop(d, q, -step, ls.at[d, q]).wait_recv()
                nxt = me + step

                @pl.when(jnp.logical_and(nxt >= 0, nxt < n))
                def _():
                    hop(d, q, step, ls.at[d, q]).start()

                cross(d, q).start()

                @pl.when(q == 0)
                def _():
                    tags(d, d).wait_recv()
                    wave(d, d).wait_recv()
                    for o in range(1, mpos):
                        wave_share(d, o).start()
                    for o in range(1, mpos):
                        wave_shared(d, o).wait_recv()
                    wave_cross(d, c).start()

    def finish(t, q):
        for step in (1, -1):
            d = me - step * t

            @pl.when(jnp.logical_and(d >= 0, d < n))
            def _():
                @pl.when(q == 0)
                def _():
                    wave_cross(d, other).wait_recv()

                cross(d, q).wait_recv()
                compute(d, q)

    def turn(u, carry):
        @pl.when(u < (n - 1) * nw)
        def _():
            arrive(u // nw + 1, lax.rem(u, nw))

        @pl.when(u > 0)
        def _():
            finish((u - 1) // nw + 1, lax.rem(u + nw - 1, nw))

        return carry

    lax.fori_loop(0, (n - 1) * nw + 1, turn, 0)

    for q in range(nw):

        @pl.when(me + 1 < n)
        def _():
            hop(me, q, 1, ls_own.at[0, q]).wait_send()

        @pl.when(me > 0)
        def _():
            hop(me, q, -1, ls_own.at[1, q]).wait_send()

    def drain(d, carry):
        wave_cross(d, c).wait_send()
        for o in range(1, mpos):
            partial_to(d, o).wait()

        @pl.when(d != me)
        def _():
            wave(d, me).wait_send()
            for o in range(1, mpos):
                wave_share(d, o).wait_send()
            tags(d, me).wait_send()
            for q in range(nw):
                cross(d, q).wait_send()

        @pl.when(jnp.logical_and(d < me, me + 1 < n))
        def _():
            for q in range(nw):
                hop(d, q, 1, ls.at[d, q]).wait_send()

        @pl.when(jnp.logical_and(d > me, me > 0))
        def _():
            for q in range(nw):
                hop(d, q, -1, ls.at[d, q]).wait_send()

        return carry

    lax.fori_loop(0, n, drain, 0)

    def emit(i, carry):
        r = recv_ref[0, i]
        d, k = r // per, lax.rem(r, per)
        value = total[d, k, own, :]
        for o in range(1, mpos):
            value = value + mbuf[o - 1, d, k].astype(F32)
        out_ref[i] = value.astype(BF)
        return carry

    lax.fori_loop(0, n * per, emit, 0)


def local(
    n,
    mpos,
    wavefunction,
    left_env,
    right_env,
    send_order,
    recv_order,
    pair_left,
    pair_right,
    left_size,
    right_size,
    mpo_pattern,
):
    pairs, width, half = wavefunction.shape
    per = pairs // n
    lefts, nw = left_env.shape[:2]
    slots = jnp.arange(pairs, dtype=jnp.int32)
    match = recv_order[0][None, :] == slots[:, None]
    right_of = jnp.sum(jnp.where(match, pair_right[0][None, :], 0), axis=1)[None, :]
    smem = pl.BlockSpec(memory_space=pltpu.SMEM)
    vmem = pl.BlockSpec(memory_space=pltpu.VMEM)
    dma = pltpu.SemaphoreType.DMA
    others = max(mpos - 1, 1)
    return pl.pallas_call(
        functools.partial(kernel, n, mpos),
        out_shape=jax.ShapeDtypeStruct((pairs, width // mpos, half), BF),
        in_specs=[smem] * 7 + [pl.BlockSpec(memory_space=pl.ANY)] * 3,
        out_specs=vmem,
        scratch_shapes=[
            pltpu.VMEM(wavefunction.shape, BF),
            pltpu.VMEM(left_env.shape, BF),
            pltpu.VMEM(right_env.shape, BF),
            dma((3,)),
            pltpu.VMEM((n, nw, lefts, width, width), BF),
            pltpu.VMEM(right_env.shape, BF),
            pltpu.VMEM((n, per, width, half), BF),
            pltpu.VMEM((n, per, lefts, 16, 128), BF),
            pltpu.VMEM((n, 2, per, width, half), BF),
            pltpu.VMEM((n, per, lefts, 16, 128), BF),
            pltpu.VMEM((n, per, width, half), F32),
            pltpu.VMEM((n, per, width, half), BF),
            pltpu.VMEM((others, n, per, width // mpos, half), BF),
            dma((2, nw)),
            dma((n, nw)),
            dma((n, nw)),
            dma((n, nw)),
            dma((n, nw)),
            dma((n,)),
            dma((n,)),
            dma((n, others)),
            dma((n, others)),
            dma((n,)),
            dma((n,)),
            dma((n,)),
            dma((n,)),
            dma((n, others)),
            dma((n, others)),
        ],
        compiler_params=pltpu.CompilerParams(
            collective_id=0, has_side_effects=True, vmem_limit_bytes=52 * 1024 * 1024
        ),
        cost_estimate=pl.CostEstimate(
            flops=6 * pairs * nw * width * width * half,
            bytes_accessed=8 * pairs * width * half,
            transcendentals=0,
        ),
        name="apply_blocks",
    )(
        send_order,
        recv_order,
        pair_left,
        right_of,
        left_size,
        right_size,
        mpo_pattern,
        wavefunction,
        left_env,
        right_env,
    )


def solution(mesh):
    placed = (
        P(("runs", "sec"), None, "rep"),
        P(("runs", "sec"), "mpo", None, None),
        P(("runs", "sec"), "mpo", None, "rep"),
        P("sec", None),
        P("sec", None),
        P("sec", None),
        P("sec", None),
        P("sec"),
        P("sec"),
        P("sec", "mpo"),
    )
    return jax.shard_map(
        functools.partial(local, mesh.shape["sec"], mesh.shape["mpo"]),
        mesh=mesh,
        in_specs=placed,
        out_specs=P(("runs", "sec"), "mpo", "rep"),
        check_vma=False,
    )
```

```python
import functools

import jax
import jax.numpy as jnp
from jax import lax
from jax.experimental import pallas as pl
from jax.experimental.pallas import tpu as pltpu
from jax.sharding import PartitionSpec as P

BF = jnp.bfloat16
F32 = jnp.float32
MESH = pl.DeviceIdType.MESH


def kernel(
    n,
    mpos,
    send_hbm,
    recv_hbm,
    pair_hbm,
    pair_right_hbm,
    lsize_hbm,
    rsize_hbm,
    pattern_hbm,
    wf_hbm,
    left_hbm,
    right_hbm,
    out_ref,
    wf_ref,
    left_ref,
    right_ref,
    load,
    send_ref,
    recv_ref,
    pair_ref,
    pair_right_ref,
    lsize_ref,
    rsize_ref,
    pattern_ref,
    right_of_ref,
    load_small,
    lbuf,
    rbuf,
    stage,
    tagstage,
    wbuf,
    tagbuf,
    total,
    rounded,
    mbuf,
    ls_own,
    ls,
    lr,
    cs,
    cr,
    ws,
    wr,
    xs,
    xr,
    vs,
    vr,
    ts,
    tr,
    ms,
    mr,
):
    me = lax.axis_index("sec")
    m = lax.axis_index("mpo")
    c = lax.axis_index("rep")
    other = 1 - c
    lefts, nw, width = left_ref.shape[:3]
    rights = right_ref.shape[0]
    half = wf_ref.shape[2]
    per = wf_ref.shape[0] // n
    part = width // 2
    mrows = width // mpos

    load_left = pltpu.make_async_copy(left_hbm, left_ref, load.at[0])
    load_wf = pltpu.make_async_copy(wf_hbm, wf_ref, load.at[1])
    load_right = pltpu.make_async_copy(right_hbm, right_ref, load.at[2])
    smalls = (
        (lsize_hbm, lsize_ref),
        (pattern_hbm, pattern_ref),
        (send_hbm, send_ref),
        (pair_hbm, pair_ref),
        (recv_hbm, recv_ref),
        (pair_right_hbm, pair_right_ref),
        (rsize_hbm, rsize_ref),
    )
    small = [pltpu.make_async_copy(a, b, load_small.at[i]) for i, (a, b) in enumerate(smalls)]
    for copy in small:
        copy.start()
    load_left.start()
    load_wf.start()
    load_right.start()
    barrier = pltpu.get_barrier_semaphore()
    for t in range(1, n):
        pl.semaphore_signal(
            barrier, inc=1, device_id={"sec": lax.rem(me + t, n)}, device_id_type=MESH
        )
    for t in range(1, mpos):
        pl.semaphore_signal(
            barrier, inc=1, device_id={"mpo": lax.rem(m + t, mpos)}, device_id_type=MESH
        )
    pl.semaphore_signal(barrier, inc=1, device_id={"rep": other}, device_id_type=MESH)

    row = lax.broadcasted_iota(jnp.int32, (width, width), 0)
    hrow = lax.broadcasted_iota(jnp.int32, (width, half), 0)
    hcol = lax.broadcasted_iota(jnp.int32, (width, half), 1) + c * half

    def my_rows(d, q):
        return lbuf.at[d, q, :, pl.ds(pl.multiple_of(c * part, part), part), :]

    def hop(d, q, step, sem):
        return pltpu.make_async_remote_copy(
            src_ref=my_rows(d, q),
            dst_ref=my_rows(d, q),
            send_sem=sem,
            recv_sem=lr.at[d, q],
            device_id={"sec": me + step},
            device_id_type=MESH,
        )

    def cross(d, q):
        return pltpu.make_async_remote_copy(
            src_ref=my_rows(d, q),
            dst_ref=my_rows(d, q),
            send_sem=cs.at[d, q],
            recv_sem=cr.at[d, q],
            device_id={"rep": other},
            device_id_type=MESH,
        )

    own = pl.ds(pl.multiple_of(m * mrows, mrows), mrows)

    def wave(e, slot):
        return pltpu.make_async_remote_copy(
            src_ref=stage.at[e, :, own, :],
            dst_ref=wbuf.at[slot, c, :, own, :],
            send_sem=ws.at[e],
            recv_sem=wr.at[slot],
            device_id={"sec": e},
            device_id_type=MESH,
        )

    def wave_share(d, o):
        return pltpu.make_async_remote_copy(
            src_ref=wbuf.at[d, c, :, own, :],
            dst_ref=wbuf.at[d, c, :, own, :],
            send_sem=xs.at[d, o - 1],
            recv_sem=xr.at[d, o - 1],
            device_id={"mpo": lax.rem(m + o, mpos)},
            device_id_type=MESH,
        )

    def wave_shared(d, o):
        source = lax.rem(m + mpos - o, mpos)
        rows = pl.ds(pl.multiple_of(source * mrows, mrows), mrows)
        return pltpu.make_async_remote_copy(
            src_ref=wbuf.at[d, c, :, rows, :],
            dst_ref=wbuf.at[d, c, :, rows, :],
            send_sem=xs.at[d, o - 1],
            recv_sem=xr.at[d, o - 1],
            device_id={"mpo": source},
            device_id_type=MESH,
        )

    def wave_cross(d, side):
        return pltpu.make_async_remote_copy(
            src_ref=wbuf.at[d, side],
            dst_ref=wbuf.at[d, side],
            send_sem=vs.at[d],
            recv_sem=vr.at[d],
            device_id={"rep": other},
            device_id_type=MESH,
        )

    def tags(e, slot):
        return pltpu.make_async_remote_copy(
            src_ref=tagstage.at[e],
            dst_ref=tagbuf.at[slot],
            send_sem=ts.at[e],
            recv_sem=tr.at[slot],
            device_id={"sec": e},
            device_id_type=MESH,
        )

    def partial_to(d, o):
        target = lax.rem(m + o, mpos)
        rows = pl.ds(pl.multiple_of(target * mrows, mrows), mrows)
        return pltpu.make_async_remote_copy(
            src_ref=rounded.at[d, :, rows, :],
            dst_ref=mbuf.at[o - 1, d],
            send_sem=ms.at[d, o - 1],
            recv_sem=mr.at[d, o - 1],
            device_id={"mpo": target},
            device_id_type=MESH,
        )

    for copy in small:
        copy.wait()
    keeps = [jnp.where(row < lsize_ref[l], 1.0, 0.0) for l in range(lefts)]
    load_left.wait()
    for q in range(nw):
        for l in range(lefts):
            scale = (keeps[l] * pattern_ref[l, q].astype(F32)).astype(BF)
            lbuf[me, q, l] = left_ref[l, q] * scale
        if q == 0:
            pl.semaphore_wait(barrier, n + mpos - 1)

        @pl.when(me + 1 < n)
        def _():
            hop(me, q, 1, ls_own.at[0, q]).start()

        @pl.when(me > 0)
        def _():
            hop(me, q, -1, ls_own.at[1, q]).start()

    load_wf.wait()

    def fill(e, carry):
        for k in range(per):
            block = send_ref[0, e * per + k]
            left = pair_ref[0, block]
            keep = jnp.where(hrow < lsize_ref[left], 1.0, 0.0).astype(BF)
            stage[e, k] = wf_ref[block] * keep
            for l in range(lefts):
                flag = jnp.where(left == l, 1.0, 0.0)
                tagstage[e, k, l] = jnp.full((16, 128), flag, F32).astype(BF)

        @pl.when(e != me)
        def _():
            tags(e, me).start()
            wave(e, me).start()

        return carry

    lax.fori_loop(0, n, fill, 0)
    wbuf[me, c] = stage[me]
    tagbuf[me] = tagstage[me]
    wave_cross(me, c).start()

    def invert(r, carry):
        b = jnp.int32(0)
        for i in range(n * per):
            b = jnp.where(recv_ref[0, i] == r, pair_right_ref[0, i], b)
        right_of_ref[r] = b
        return carry

    lax.fori_loop(0, n * per, invert, 0)

    load_right.wait()
    for b in range(rights):
        size = rsize_ref[b]
        keep = jnp.where(jnp.logical_and(hrow < size, hcol < size), 1.0, 0.0).astype(BF)
        for w in range(nw):
            rbuf[b, w] = right_ref[b, w] * keep

    def compute(d, q):
        for k in range(per):
            x = jnp.concatenate([wbuf[d, 0, k], wbuf[d, 1, k]], axis=1)
            b = right_of_ref[d * per + k]
            env = None
            for l in range(lefts):
                flag = tagbuf[d, k, l]
                flag = jnp.concatenate([flag] * (width // 128), axis=1)
                flag = jnp.concatenate([flag] * (width // 16), axis=0)
                term = lbuf[d, q, l] * flag
                env = term if env is None else env + term
            y = jnp.dot(env, x, preferred_element_type=F32).astype(BF)
            total[d, k] += jnp.dot(y, rbuf[b, q], preferred_element_type=F32)

        @pl.when(q == nw - 1)
        def _():
            for k in range(per):
                rounded[d, k] = total[d, k].astype(BF)
            for o in range(1, mpos):
                partial_to(d, o).start()

    def clear(d, carry):
        for k in range(per):
            total[d, k] = jnp.zeros((width, half), F32)
        return carry

    lax.fori_loop(0, n, clear, 0)

    wave_cross(me, other).wait_recv()

    def first(q, carry):
        compute(me, q)
        return carry

    lax.fori_loop(0, nw, first, 0)

    def arrive(t, q):
        for step in (1, -1):
            d = me - step * t

            @pl.when(jnp.logical_and(d >= 0, d < n))
            def _():
                hop(d, q, -step, ls.at[d, q]).wait_recv()
                nxt = me + step

                @pl.when(jnp.logical_and(nxt >= 0, nxt < n))
                def _():
                    hop(d, q, step, ls.at[d, q]).start()

                cross(d, q).start()

                @pl.when(q == 0)
                def _():
                    tags(d, d).wait_recv()
                    wave(d, d).wait_recv()
                    for o in range(1, mpos):
                        wave_share(d, o).start()
                    for o in range(1, mpos):
                        wave_shared(d, o).wait_recv()
                    wave_cross(d, c).start()

    def finish(t, q):
        for step in (1, -1):
            d = me - step * t

            @pl.when(jnp.logical_and(d >= 0, d < n))
            def _():
                @pl.when(q == 0)
                def _():
                    wave_cross(d, other).wait_recv()

                cross(d, q).wait_recv()
                compute(d, q)

    def turn(u, carry):
        @pl.when(u < (n - 1) * nw)
        def _():
            arrive(u // nw + 1, lax.rem(u, nw))

        @pl.when(u > 0)
        def _():
            finish((u - 1) // nw + 1, lax.rem(u + nw - 1, nw))

        return carry

    lax.fori_loop(0, (n - 1) * nw + 1, turn, 0)

    for q in range(nw):

        @pl.when(me + 1 < n)
        def _():
            hop(me, q, 1, ls_own.at[0, q]).wait_send()

        @pl.when(me > 0)
        def _():
            hop(me, q, -1, ls_own.at[1, q]).wait_send()

    def drain(d, carry):
        wave_cross(d, c).wait_send()
        for o in range(1, mpos):
            partial_to(d, o).wait()

        @pl.when(d != me)
        def _():
            wave(d, me).wait_send()
            for o in range(1, mpos):
                wave_share(d, o).wait_send()
            tags(d, me).wait_send()
            for q in range(nw):
                cross(d, q).wait_send()

        @pl.when(jnp.logical_and(d < me, me + 1 < n))
        def _():
            for q in range(nw):
                hop(d, q, 1, ls.at[d, q]).wait_send()

        @pl.when(jnp.logical_and(d > me, me > 0))
        def _():
            for q in range(nw):
                hop(d, q, -1, ls.at[d, q]).wait_send()

        return carry

    lax.fori_loop(0, n, drain, 0)

    def emit(i, carry):
        r = recv_ref[0, i]
        d, k = r // per, lax.rem(r, per)
        value = total[d, k, own, :]
        for o in range(1, mpos):
            value = value + mbuf[o - 1, d, k].astype(F32)
        out_ref[i] = value.astype(BF)
        return carry

    lax.fori_loop(0, n * per, emit, 0)


def local(
    n,
    mpos,
    wavefunction,
    left_env,
    right_env,
    send_order,
    recv_order,
    pair_left,
    pair_right,
    left_size,
    right_size,
    mpo_pattern,
):
    pairs, width, half = wavefunction.shape
    per = pairs // n
    lefts, nw = left_env.shape[:2]
    vmem = pl.BlockSpec(memory_space=pltpu.VMEM)
    dma = pltpu.SemaphoreType.DMA
    others = max(mpos - 1, 1)
    return pl.pallas_call(
        functools.partial(kernel, n, mpos),
        out_shape=jax.ShapeDtypeStruct((pairs, width // mpos, half), BF),
        in_specs=[pl.BlockSpec(memory_space=pl.ANY)] * 10,
        out_specs=vmem,
        scratch_shapes=[
            pltpu.VMEM(wavefunction.shape, BF),
            pltpu.VMEM(left_env.shape, BF),
            pltpu.VMEM(right_env.shape, BF),
            dma((3,)),
            pltpu.SMEM(send_order.shape, jnp.int32),
            pltpu.SMEM(recv_order.shape, jnp.int32),
            pltpu.SMEM(pair_left.shape, jnp.int32),
            pltpu.SMEM(pair_right.shape, jnp.int32),
            pltpu.SMEM(left_size.shape, jnp.int32),
            pltpu.SMEM(right_size.shape, jnp.int32),
            pltpu.SMEM(mpo_pattern.shape, jnp.int32),
            pltpu.SMEM((pairs,), jnp.int32),
            dma((7,)),
            pltpu.VMEM((n, nw, lefts, width, width), BF),
            pltpu.VMEM(right_env.shape, BF),
            pltpu.VMEM((n, per, width, half), BF),
            pltpu.VMEM((n, per, lefts, 16, 128), BF),
            pltpu.VMEM((n, 2, per, width, half), BF),
            pltpu.VMEM((n, per, lefts, 16, 128), BF),
            pltpu.VMEM((n, per, width, half), F32),
            pltpu.VMEM((n, per, width, half), BF),
            pltpu.VMEM((others, n, per, width // mpos, half), BF),
            dma((2, nw)),
            dma((n, nw)),
            dma((n, nw)),
            dma((n, nw)),
            dma((n, nw)),
            dma((n,)),
            dma((n,)),
            dma((n, others)),
            dma((n, others)),
            dma((n,)),
            dma((n,)),
            dma((n,)),
            dma((n,)),
            dma((n, others)),
            dma((n, others)),
        ],
        compiler_params=pltpu.CompilerParams(
            collective_id=0, has_side_effects=True, vmem_limit_bytes=52 * 1024 * 1024
        ),
        cost_estimate=pl.CostEstimate(
            flops=6 * pairs * nw * width * width * half,
            bytes_accessed=8 * pairs * width * half,
            transcendentals=0,
        ),
        name="apply_blocks",
    )(
        send_order,
        recv_order,
        pair_left,
        pair_right,
        left_size,
        right_size,
        mpo_pattern,
        wavefunction,
        left_env,
        right_env,
    )


def solution(mesh):
    placed = (
        P(("runs", "sec"), None, "rep"),
        P(("runs", "sec"), "mpo", None, None),
        P(("runs", "sec"), "mpo", None, "rep"),
        P("sec", None),
        P("sec", None),
        P("sec", None),
        P("sec", None),
        P("sec"),
        P("sec"),
        P("sec", "mpo"),
    )
    return jax.shard_map(
        functools.partial(local, mesh.shape["sec"], mesh.shape["mpo"]),
        mesh=mesh,
        in_specs=placed,
        out_specs=P(("runs", "sec"), "mpo", "rep"),
        check_vma=False,
    )
```

```python
import functools

import jax
import jax.numpy as jnp
from jax import lax
from jax.experimental import pallas as pl
from jax.experimental.pallas import tpu as pltpu
from jax.sharding import PartitionSpec as P

BF = jnp.bfloat16
F32 = jnp.float32
MESH = pl.DeviceIdType.MESH


def kernel(
    n,
    mpos,
    send_hbm,
    recv_hbm,
    pair_hbm,
    pair_right_hbm,
    lsize_hbm,
    rsize_hbm,
    pattern_hbm,
    wf_hbm,
    left_hbm,
    right_hbm,
    out_ref,
    wf_ref,
    left_ref,
    right_ref,
    load,
    send_ref,
    recv_ref,
    pair_ref,
    pair_right_ref,
    lsize_ref,
    rsize_ref,
    pattern_ref,
    right_of_ref,
    load_small,
    lbuf,
    rbuf,
    stage,
    tagstage,
    wbuf,
    tagbuf,
    total,
    rounded,
    mbuf,
    ls_own,
    ls,
    lr,
    cs,
    cr,
    ws,
    wr,
    xs,
    xr,
    vs,
    vr,
    ts,
    tr,
    ms,
    mr,
    rx,
    rtagstage,
    rtag,
    fstage,
    fbuf,
    es,
    er,
):
    me = lax.axis_index("sec")
    m = lax.axis_index("mpo")
    c = lax.axis_index("rep")
    other = 1 - c
    last = n - 1
    proxied = n >= 4
    is_end = jnp.logical_or(me == 0, me == last)
    is_proxy = jnp.logical_or(me == 1, me == last - 1)
    helper = jnp.where(me == 0, 1, last - 1)
    end = jnp.where(me == 1, 0, last)
    far = last - jnp.where(is_end, me, end)

    def moved(d, e):
        if not proxied:
            return d < 0
        low = jnp.logical_and(d == last, e == 0)
        return jnp.logical_or(low, jnp.logical_and(d == 0, e == last))

    def both(*terms):
        return functools.reduce(jnp.logical_and, terms)

    lefts, nw, width = left_ref.shape[:3]
    rights = right_ref.shape[0]
    half = wf_ref.shape[2]
    per = wf_ref.shape[0] // n
    part = width // 2
    mrows = width // mpos

    load_left = pltpu.make_async_copy(left_hbm, left_ref, load.at[0])
    load_wf = pltpu.make_async_copy(wf_hbm, wf_ref, load.at[1])
    load_right = pltpu.make_async_copy(right_hbm, right_ref, load.at[2])
    smalls = (
        (lsize_hbm, lsize_ref),
        (pattern_hbm, pattern_ref),
        (send_hbm, send_ref),
        (pair_hbm, pair_ref),
        (recv_hbm, recv_ref),
        (pair_right_hbm, pair_right_ref),
        (rsize_hbm, rsize_ref),
    )
    small = [pltpu.make_async_copy(a, b, load_small.at[i]) for i, (a, b) in enumerate(smalls)]
    for copy in small:
        copy.start()
    load_left.start()
    load_wf.start()
    load_right.start()
    barrier = pltpu.get_barrier_semaphore()
    for t in range(1, n):
        pl.semaphore_signal(
            barrier, inc=1, device_id={"sec": lax.rem(me + t, n)}, device_id_type=MESH
        )
    for t in range(1, mpos):
        pl.semaphore_signal(
            barrier, inc=1, device_id={"mpo": lax.rem(m + t, mpos)}, device_id_type=MESH
        )
    pl.semaphore_signal(barrier, inc=1, device_id={"rep": other}, device_id_type=MESH)

    row = lax.broadcasted_iota(jnp.int32, (width, width), 0)
    hrow = lax.broadcasted_iota(jnp.int32, (width, half), 0)
    hcol = lax.broadcasted_iota(jnp.int32, (width, half), 1) + c * half

    def my_rows(d, q):
        return lbuf.at[d, q, :, pl.ds(pl.multiple_of(c * part, part), part), :]

    def hop(d, q, step, sem):
        return pltpu.make_async_remote_copy(
            src_ref=my_rows(d, q),
            dst_ref=my_rows(d, q),
            send_sem=sem,
            recv_sem=lr.at[d, q],
            device_id={"sec": me + step},
            device_id_type=MESH,
        )

    def cross(d, q):
        return pltpu.make_async_remote_copy(
            src_ref=my_rows(d, q),
            dst_ref=my_rows(d, q),
            send_sem=cs.at[d, q],
            recv_sem=cr.at[d, q],
            device_id={"rep": other},
            device_id_type=MESH,
        )

    own = pl.ds(pl.multiple_of(m * mrows, mrows), mrows)

    def wave(e, slot, device):
        return pltpu.make_async_remote_copy(
            src_ref=stage.at[e, :, own, :],
            dst_ref=wbuf.at[slot, c, :, own, :],
            send_sem=ws.at[e],
            recv_sem=wr.at[slot],
            device_id={"sec": device},
            device_id_type=MESH,
        )

    def wave_share(d, o):
        return pltpu.make_async_remote_copy(
            src_ref=wbuf.at[d, c, :, own, :],
            dst_ref=wbuf.at[d, c, :, own, :],
            send_sem=xs.at[d, o - 1],
            recv_sem=xr.at[d, o - 1],
            device_id={"mpo": lax.rem(m + o, mpos)},
            device_id_type=MESH,
        )

    def wave_shared(d, o):
        source = lax.rem(m + mpos - o, mpos)
        rows = pl.ds(pl.multiple_of(source * mrows, mrows), mrows)
        return pltpu.make_async_remote_copy(
            src_ref=wbuf.at[d, c, :, rows, :],
            dst_ref=wbuf.at[d, c, :, rows, :],
            send_sem=xs.at[d, o - 1],
            recv_sem=xr.at[d, o - 1],
            device_id={"mpo": source},
            device_id_type=MESH,
        )

    def wave_cross(d, side):
        return pltpu.make_async_remote_copy(
            src_ref=wbuf.at[d, side],
            dst_ref=wbuf.at[d, side],
            send_sem=vs.at[d],
            recv_sem=vr.at[d],
            device_id={"rep": other},
            device_id_type=MESH,
        )

    def tags(e, slot, device):
        return pltpu.make_async_remote_copy(
            src_ref=tagstage.at[e],
            dst_ref=tagbuf.at[slot],
            send_sem=ts.at[e],
            recv_sem=tr.at[slot],
            device_id={"sec": device},
            device_id_type=MESH,
        )

    def partial_to(d, o):
        target = lax.rem(m + o, mpos)
        rows = pl.ds(pl.multiple_of(target * mrows, mrows), mrows)
        return pltpu.make_async_remote_copy(
            src_ref=rounded.at[d, :, rows, :],
            dst_ref=mbuf.at[o - 1, d],
            send_sem=ms.at[d, o - 1],
            recv_sem=mr.at[d, o - 1],
            device_id={"mpo": target},
            device_id_type=MESH,
        )

    for copy in small:
        copy.wait()
    keeps = [jnp.where(row < lsize_ref[l], 1.0, 0.0) for l in range(lefts)]
    load_left.wait()
    for q in range(nw):
        for l in range(lefts):
            scale = (keeps[l] * pattern_ref[l, q].astype(F32)).astype(BF)
            lbuf[me, q, l] = left_ref[l, q] * scale
        if q == 0:
            pl.semaphore_wait(barrier, n + mpos - 1)

        @pl.when(me + 1 < n)
        def _():
            hop(me, q, 1, ls_own.at[0, q]).start()

        @pl.when(me > 0)
        def _():
            hop(me, q, -1, ls_own.at[1, q]).start()

    load_wf.wait()

    def fill(e, carry):
        for k in range(per):
            block = send_ref[0, e * per + k]
            left = pair_ref[0, block]
            keep = jnp.where(hrow < lsize_ref[left], 1.0, 0.0).astype(BF)
            stage[e, k] = wf_ref[block] * keep
            for l in range(lefts):
                flag = jnp.where(left == l, 1.0, 0.0)
                tagstage[e, k, l] = jnp.full((16, 128), flag, F32).astype(BF)

        @pl.when(e != me)
        def _():
            away = moved(me, e)
            slot = jnp.where(away, n, me)
            device = jnp.where(away, jnp.where(e == 0, 1, last - 1), e)
            tags(e, slot, device).start()
            wave(e, slot, device).start()

        return carry

    lax.fori_loop(0, n, fill, 0)
    wbuf[me, c] = stage[me]
    tagbuf[me] = tagstage[me]
    wave_cross(me, c).start()

    def invert(r, carry):
        b = jnp.int32(0)
        for i in range(n * per):
            b = jnp.where(recv_ref[0, i] == r, pair_right_ref[0, i], b)
        right_of_ref[r] = b
        return carry

    lax.fori_loop(0, n * per, invert, 0)

    load_right.wait()
    for b in range(rights):
        size = rsize_ref[b]
        keep = jnp.where(jnp.logical_and(hrow < size, hcol < size), 1.0, 0.0).astype(BF)
        for w in range(nw):
            rbuf[b, w] = right_ref[b, w] * keep

    def to_helper(i, source, target, device):
        return pltpu.make_async_remote_copy(
            src_ref=source,
            dst_ref=target,
            send_sem=es.at[i],
            recv_sem=er.at[i],
            device_id={"sec": device},
            device_id_type=MESH,
        )

    def helper_copies(device):
        return to_helper(0, rbuf, rx, device), to_helper(1, rtagstage, rtag, device)

    def result_copy(device):
        return to_helper(2, fstage, fbuf, device)

    if proxied:

        @pl.when(is_end)
        def _():
            for k in range(per):
                right = right_of_ref[far * per + k]
                for b in range(rights):
                    flag = jnp.where(right == b, 1.0, 0.0)
                    rtagstage[k, b] = jnp.full((16, 128), flag, F32).astype(BF)
            for copy in helper_copies(helper):
                copy.start()

    def spread(flag, columns):
        flag = jnp.concatenate([flag] * (columns // 128), axis=1)
        return jnp.concatenate([flag] * (width // 16), axis=0)

    def compute_moved(q):
        for k in range(per):
            x = jnp.concatenate([wbuf[n, 0, k], wbuf[n, 1, k]], axis=1)
            env = lbuf[far, q, 0] * spread(tagbuf[n, k, 0], width)
            for l in range(1, lefts):
                env = env + lbuf[far, q, l] * spread(tagbuf[n, k, l], width)
            renv = rx[0, q] * spread(rtag[k, 0], half)
            for b in range(1, rights):
                renv = renv + rx[b, q] * spread(rtag[k, b], half)
            y = jnp.dot(env, x, preferred_element_type=F32).astype(BF)
            total[n, k] += jnp.dot(y, renv, preferred_element_type=F32)

        @pl.when(q == nw - 1)
        def _():
            for k in range(per):
                rounded[n, k] = total[n, k].astype(BF)
            for o in range(1, mpos):
                partial_to(n, o).start()

    def compute(d, q):
        for k in range(per):
            x = jnp.concatenate([wbuf[d, 0, k], wbuf[d, 1, k]], axis=1)
            b = right_of_ref[d * per + k]
            env = None
            for l in range(lefts):
                flag = tagbuf[d, k, l]
                flag = jnp.concatenate([flag] * (width // 128), axis=1)
                flag = jnp.concatenate([flag] * (width // 16), axis=0)
                term = lbuf[d, q, l] * flag
                env = term if env is None else env + term
            y = jnp.dot(env, x, preferred_element_type=F32).astype(BF)
            total[d, k] += jnp.dot(y, rbuf[b, q], preferred_element_type=F32)

        @pl.when(q == nw - 1)
        def _():
            for k in range(per):
                rounded[d, k] = total[d, k].astype(BF)
            for o in range(1, mpos):
                partial_to(d, o).start()

    def clear(d, carry):
        for k in range(per):
            total[d, k] = jnp.zeros((width, half), F32)
        return carry

    lax.fori_loop(0, n + 1 if proxied else n, clear, 0)

    wave_cross(me, other).wait_recv()

    def first(q, carry):
        compute(me, q)
        return carry

    lax.fori_loop(0, nw, first, 0)

    def receive(d, slot):
        tags(d, slot, d).wait_recv()
        wave(d, slot, d).wait_recv()
        for o in range(1, mpos):
            wave_share(slot, o).start()
        for o in range(1, mpos):
            wave_shared(slot, o).wait_recv()
        wave_cross(slot, c).start()

    def arrive(t, q):
        for step in (1, -1):
            d = me - step * t

            @pl.when(both(d >= 0, d < n, jnp.logical_not(moved(d, me))))
            def _():
                hop(d, q, -step, ls.at[d, q]).wait_recv()
                nxt = me + step

                @pl.when(both(nxt >= 0, nxt < n, jnp.logical_not(moved(d, nxt))))
                def _():
                    hop(d, q, step, ls.at[d, q]).start()

                cross(d, q).start()

                @pl.when(q == 0)
                def _():
                    receive(d, d)

                if proxied:

                    @pl.when(both(q == 0, is_proxy, d == far))
                    def _():
                        receive(d, n)

    def finish(t, q):
        for step in (1, -1):
            d = me - step * t

            @pl.when(both(d >= 0, d < n, jnp.logical_not(moved(d, me))))
            def _():
                @pl.when(q == 0)
                def _():
                    wave_cross(d, other).wait_recv()

                cross(d, q).wait_recv()
                compute(d, q)

                if proxied:

                    @pl.when(both(is_proxy, d == far))
                    def _():
                        @pl.when(q == 0)
                        def _():
                            wave_cross(n, other).wait_recv()
                            for copy in helper_copies(end):
                                copy.wait_recv()

                        compute_moved(q)

    def turn(u, carry):
        @pl.when(u < (n - 1) * nw)
        def _():
            arrive(u // nw + 1, lax.rem(u, nw))

        @pl.when(u > 0)
        def _():
            finish((u - 1) // nw + 1, lax.rem(u + nw - 1, nw))

        return carry

    lax.fori_loop(0, (n - 1) * nw + 1, turn, 0)

    if proxied:

        @pl.when(is_proxy)
        def _():
            for o in range(1, mpos):
                partial_to(n, o).wait_recv()
            for k in range(per):
                value = total[n, k, own, :]
                for o in range(1, mpos):
                    value = value + mbuf[o - 1, n, k].astype(F32)
                fstage[k] = value.astype(BF)
            result_copy(end).start()
            wave_cross(n, c).wait_send()
            for o in range(1, mpos):
                partial_to(n, o).wait_send()
                wave_share(n, o).wait_send()
            result_copy(end).wait_send()

        @pl.when(is_end)
        def _():
            for copy in helper_copies(helper):
                copy.wait_send()
            result_copy(helper).wait_recv()
            for k in range(per):
                total[far, k, own, :] = fbuf[k].astype(F32)
                for o in range(1, mpos):
                    mbuf[o - 1, far, k] = jnp.zeros((mrows, half), BF)

    for q in range(nw):

        @pl.when(me + 1 < n)
        def _():
            hop(me, q, 1, ls_own.at[0, q]).wait_send()

        @pl.when(me > 0)
        def _():
            hop(me, q, -1, ls_own.at[1, q]).wait_send()

    def drain(d, carry):
        @pl.when(jnp.logical_not(moved(d, me)))
        def _():
            wave_cross(d, c).wait_send()
            for o in range(1, mpos):
                partial_to(d, o).wait()

        @pl.when(d != me)
        def _():
            wave(d, me, d).wait_send()
            tags(d, me, d).wait_send()

        @pl.when(both(d != me, jnp.logical_not(moved(d, me))))
        def _():
            for o in range(1, mpos):
                wave_share(d, o).wait_send()
            for q in range(nw):
                cross(d, q).wait_send()

        @pl.when(both(d < me, me + 1 < n, jnp.logical_not(moved(d, me + 1))))
        def _():
            for q in range(nw):
                hop(d, q, 1, ls.at[d, q]).wait_send()

        @pl.when(both(d > me, me > 0, jnp.logical_not(moved(d, me - 1))))
        def _():
            for q in range(nw):
                hop(d, q, -1, ls.at[d, q]).wait_send()

        return carry

    lax.fori_loop(0, n, drain, 0)

    def emit(i, carry):
        r = recv_ref[0, i]
        d, k = r // per, lax.rem(r, per)
        value = total[d, k, own, :]
        for o in range(1, mpos):
            value = value + mbuf[o - 1, d, k].astype(F32)
        out_ref[i] = value.astype(BF)
        return carry

    lax.fori_loop(0, n * per, emit, 0)


def local(
    n,
    mpos,
    wavefunction,
    left_env,
    right_env,
    send_order,
    recv_order,
    pair_left,
    pair_right,
    left_size,
    right_size,
    mpo_pattern,
):
    pairs, width, half = wavefunction.shape
    per = pairs // n
    lefts, nw = left_env.shape[:2]
    vmem = pl.BlockSpec(memory_space=pltpu.VMEM)
    dma = pltpu.SemaphoreType.DMA
    others = max(mpos - 1, 1)
    return pl.pallas_call(
        functools.partial(kernel, n, mpos),
        out_shape=jax.ShapeDtypeStruct((pairs, width // mpos, half), BF),
        in_specs=[pl.BlockSpec(memory_space=pltpu.HBM)] * 10,
        out_specs=vmem,
        scratch_shapes=[
            pltpu.VMEM(wavefunction.shape, BF),
            pltpu.VMEM(left_env.shape, BF),
            pltpu.VMEM(right_env.shape, BF),
            dma((3,)),
            pltpu.SMEM(send_order.shape, jnp.int32),
            pltpu.SMEM(recv_order.shape, jnp.int32),
            pltpu.SMEM(pair_left.shape, jnp.int32),
            pltpu.SMEM(pair_right.shape, jnp.int32),
            pltpu.SMEM(left_size.shape, jnp.int32),
            pltpu.SMEM(right_size.shape, jnp.int32),
            pltpu.SMEM(mpo_pattern.shape, jnp.int32),
            pltpu.SMEM((pairs,), jnp.int32),
            dma((7,)),
            pltpu.VMEM((n, nw, lefts, width, width), BF),
            pltpu.VMEM(right_env.shape, BF),
            pltpu.VMEM((n, per, width, half), BF),
            pltpu.VMEM((n, per, lefts, 16, 128), BF),
            pltpu.VMEM((n + 1, 2, per, width, half), BF),
            pltpu.VMEM((n + 1, per, lefts, 16, 128), BF),
            pltpu.VMEM((n + 1, per, width, half), F32),
            pltpu.VMEM((n + 1, per, width, half), BF),
            pltpu.VMEM((others, n + 1, per, width // mpos, half), BF),
            dma((2, nw)),
            dma((n, nw)),
            dma((n, nw)),
            dma((n, nw)),
            dma((n, nw)),
            dma((n + 1,)),
            dma((n + 1,)),
            dma((n + 1, others)),
            dma((n + 1, others)),
            dma((n + 1,)),
            dma((n + 1,)),
            dma((n + 1,)),
            dma((n + 1,)),
            dma((n + 1, others)),
            dma((n + 1, others)),
            pltpu.VMEM(right_env.shape, BF),
            pltpu.VMEM((per, right_env.shape[0], 16, 128), BF),
            pltpu.VMEM((per, right_env.shape[0], 16, 128), BF),
            pltpu.VMEM((per, width // mpos, half), BF),
            pltpu.VMEM((per, width // mpos, half), BF),
            dma((3,)),
            dma((3,)),
        ],
        compiler_params=pltpu.CompilerParams(
            collective_id=0, has_side_effects=True, vmem_limit_bytes=52 * 1024 * 1024
        ),
        cost_estimate=pl.CostEstimate(
            flops=6 * pairs * nw * width * width * half,
            bytes_accessed=8 * pairs * width * half,
            transcendentals=0,
        ),
        name="apply_blocks",
    )(
        send_order,
        recv_order,
        pair_left,
        pair_right,
        left_size,
        right_size,
        mpo_pattern,
        wavefunction,
        left_env,
        right_env,
    )


def solution(mesh):
    placed = (
        P(("runs", "sec"), None, "rep"),
        P(("runs", "sec"), "mpo", None, None),
        P(("runs", "sec"), "mpo", None, "rep"),
        P("sec", None),
        P("sec", None),
        P("sec", None),
        P("sec", None),
        P("sec"),
        P("sec"),
        P("sec", "mpo"),
    )
    return jax.shard_map(
        functools.partial(local, mesh.shape["sec"], mesh.shape["mpo"]),
        mesh=mesh,
        in_specs=placed,
        out_specs=P(("runs", "sec"), "mpo", "rep"),
        check_vma=False,
    )
```

```python
import functools

import jax
import jax.numpy as jnp
from jax import lax
from jax.experimental import pallas as pl
from jax.experimental.pallas import tpu as pltpu
from jax.sharding import PartitionSpec as P

BF = jnp.bfloat16
F32 = jnp.float32
MESH = pl.DeviceIdType.MESH


def kernel(
    n,
    mpos,
    send_hbm,
    recv_hbm,
    pair_hbm,
    pair_right_hbm,
    lsize_hbm,
    rsize_hbm,
    pattern_hbm,
    wf_hbm,
    left_hbm,
    right_hbm,
    out_ref,
    wf_ref,
    left_ref,
    right_ref,
    load,
    send_ref,
    recv_ref,
    pair_ref,
    pair_right_ref,
    lsize_ref,
    rsize_ref,
    pattern_ref,
    right_of_ref,
    load_small,
    lbuf,
    rbuf,
    stage,
    tagstage,
    wbuf,
    tagbuf,
    total,
    rounded,
    mbuf,
    ls_own,
    ls,
    lr,
    cs,
    cr,
    ws,
    wr,
    xs,
    xr,
    vs,
    vr,
    ts,
    tr,
    ms,
    mr,
):
    me = lax.axis_index("sec")
    m = lax.axis_index("mpo")
    c = lax.axis_index("rep")
    other = 1 - c
    lefts, nw, width = left_ref.shape[:3]
    rights = right_ref.shape[0]
    half = wf_ref.shape[2]
    per = wf_ref.shape[0] // n
    part = width // 2
    mrows = width // mpos

    load_left = pltpu.make_async_copy(left_hbm, left_ref, load.at[0])
    load_wf = pltpu.make_async_copy(wf_hbm, wf_ref, load.at[1])
    load_right = pltpu.make_async_copy(right_hbm, right_ref, load.at[2])
    smalls = (
        (lsize_hbm, lsize_ref),
        (pattern_hbm, pattern_ref),
        (send_hbm, send_ref),
        (pair_hbm, pair_ref),
        (recv_hbm, recv_ref),
        (pair_right_hbm, pair_right_ref),
        (rsize_hbm, rsize_ref),
    )
    small = [pltpu.make_async_copy(a, b, load_small.at[i]) for i, (a, b) in enumerate(smalls)]
    for copy in small:
        copy.start()
    load_left.start()
    load_wf.start()
    load_right.start()
    barrier = pltpu.get_barrier_semaphore()
    for t in range(1, n):
        pl.semaphore_signal(
            barrier, inc=1, device_id={"sec": lax.rem(me + t, n)}, device_id_type=MESH
        )
    for t in range(1, mpos):
        pl.semaphore_signal(
            barrier, inc=1, device_id={"mpo": lax.rem(m + t, mpos)}, device_id_type=MESH
        )
    pl.semaphore_signal(barrier, inc=1, device_id={"rep": other}, device_id_type=MESH)

    row = lax.broadcasted_iota(jnp.int32, (width, width), 0)
    hrow = lax.broadcasted_iota(jnp.int32, (width, half), 0)
    hcol = lax.broadcasted_iota(jnp.int32, (width, half), 1) + c * half

    def my_rows(d, q):
        return lbuf.at[d, q, :, pl.ds(pl.multiple_of(c * part, part), part), :]

    def hop(d, q, step, sem):
        return pltpu.make_async_remote_copy(
            src_ref=my_rows(d, q),
            dst_ref=my_rows(d, q),
            send_sem=sem,
            recv_sem=lr.at[d, q],
            device_id={"sec": me + step},
            device_id_type=MESH,
        )

    def cross(d, q):
        return pltpu.make_async_remote_copy(
            src_ref=my_rows(d, q),
            dst_ref=my_rows(d, q),
            send_sem=cs.at[d, q],
            recv_sem=cr.at[d, q],
            device_id={"rep": other},
            device_id_type=MESH,
        )

    own = pl.ds(pl.multiple_of(m * mrows, mrows), mrows)

    def wave(e, slot):
        return pltpu.make_async_remote_copy(
            src_ref=stage.at[e, :, own, :],
            dst_ref=wbuf.at[slot, c, :, own, :],
            send_sem=ws.at[e],
            recv_sem=wr.at[slot],
            device_id={"sec": e},
            device_id_type=MESH,
        )

    def wave_share(d, o):
        return pltpu.make_async_remote_copy(
            src_ref=wbuf.at[d, c, :, own, :],
            dst_ref=wbuf.at[d, c, :, own, :],
            send_sem=xs.at[d, o - 1],
            recv_sem=xr.at[d, o - 1],
            device_id={"mpo": lax.rem(m + o, mpos)},
            device_id_type=MESH,
        )

    def wave_shared(d, o):
        source = lax.rem(m + mpos - o, mpos)
        rows = pl.ds(pl.multiple_of(source * mrows, mrows), mrows)
        return pltpu.make_async_remote_copy(
            src_ref=wbuf.at[d, c, :, rows, :],
            dst_ref=wbuf.at[d, c, :, rows, :],
            send_sem=xs.at[d, o - 1],
            recv_sem=xr.at[d, o - 1],
            device_id={"mpo": source},
            device_id_type=MESH,
        )

    def wave_cross(d, side):
        return pltpu.make_async_remote_copy(
            src_ref=wbuf.at[d, side],
            dst_ref=wbuf.at[d, side],
            send_sem=vs.at[d],
            recv_sem=vr.at[d],
            device_id={"rep": other},
            device_id_type=MESH,
        )

    def tags(e, slot):
        return pltpu.make_async_remote_copy(
            src_ref=tagstage.at[e],
            dst_ref=tagbuf.at[slot],
            send_sem=ts.at[e],
            recv_sem=tr.at[slot],
            device_id={"sec": e},
            device_id_type=MESH,
        )

    def partial_to(d, o):
        target = lax.rem(m + o, mpos)
        rows = pl.ds(pl.multiple_of(target * mrows, mrows), mrows)
        return pltpu.make_async_remote_copy(
            src_ref=rounded.at[d, :, rows, :],
            dst_ref=mbuf.at[o - 1, d],
            send_sem=ms.at[d, o - 1],
            recv_sem=mr.at[d, o - 1],
            device_id={"mpo": target},
            device_id_type=MESH,
        )

    for copy in small:
        copy.wait()
    keeps = [jnp.where(row < lsize_ref[l], 1.0, 0.0) for l in range(lefts)]
    load_left.wait()
    for q in range(nw):
        for l in range(lefts):
            scale = (keeps[l] * pattern_ref[l, q].astype(F32)).astype(BF)
            lbuf[me, q, l] = left_ref[l, q] * scale
        if q == 0:
            pl.semaphore_wait(barrier, n + mpos - 1)

        @pl.when(me + 1 < n)
        def _():
            hop(me, q, 1, ls_own.at[0, q]).start()

        @pl.when(me > 0)
        def _():
            hop(me, q, -1, ls_own.at[1, q]).start()

    load_wf.wait()

    def fill(e, carry):
        for k in range(per):
            block = send_ref[0, e * per + k]
            left = pair_ref[0, block]
            keep = jnp.where(hrow < lsize_ref[left], 1.0, 0.0).astype(BF)
            stage[e, k] = wf_ref[block] * keep
            for l in range(lefts):
                flag = jnp.where(left == l, 1.0, 0.0)
                tagstage[e, k, l] = jnp.full((16, 128), flag, F32).astype(BF)

        @pl.when(e != me)
        def _():
            tags(e, me).start()
            wave(e, me).start()

        return carry

    lax.fori_loop(0, n, fill, 0)
    wbuf[me, c] = stage[me]
    tagbuf[me] = tagstage[me]
    wave_cross(me, c).start()

    def invert(r, carry):
        b = jnp.int32(0)
        for i in range(n * per):
            b = jnp.where(recv_ref[0, i] == r, pair_right_ref[0, i], b)
        right_of_ref[r] = b
        return carry

    lax.fori_loop(0, n * per, invert, 0)

    load_right.wait()
    for b in range(rights):
        size = rsize_ref[b]
        keep = jnp.where(jnp.logical_and(hrow < size, hcol < size), 1.0, 0.0).astype(BF)
        for w in range(nw):
            rbuf[b, w] = right_ref[b, w] * keep

    def compute(d, q):
        for k in range(per):
            x = jnp.concatenate([wbuf[d, 0, k], wbuf[d, 1, k]], axis=1)
            b = right_of_ref[d * per + k]
            env = None
            for l in range(lefts):
                flag = tagbuf[d, k, l]
                flag = jnp.concatenate([flag] * (width // 128), axis=1)
                flag = jnp.concatenate([flag] * (width // 16), axis=0)
                term = lbuf[d, q, l] * flag
                env = term if env is None else env + term
            y = jnp.dot(env, x, preferred_element_type=F32).astype(BF)
            total[d, k] += jnp.dot(y, rbuf[b, q], preferred_element_type=F32)

        @pl.when(q == nw - 1)
        def _():
            for k in range(per):
                rounded[d, k] = total[d, k].astype(BF)
            for o in range(1, mpos):
                partial_to(d, o).start()

    def clear(d, carry):
        for k in range(per):
            total[d, k] = jnp.zeros((width, half), F32)
        return carry

    lax.fori_loop(0, n, clear, 0)

    wave_cross(me, other).wait_recv()

    def first(q, carry):
        compute(me, q)
        return carry

    lax.fori_loop(0, nw, first, 0)

    def arrive(t, q):
        for step in (1, -1):
            d = me - step * t

            @pl.when(jnp.logical_and(d >= 0, d < n))
            def _():
                hop(d, q, -step, ls.at[d, q]).wait_recv()
                nxt = me + step

                @pl.when(jnp.logical_and(nxt >= 0, nxt < n))
                def _():
                    hop(d, q, step, ls.at[d, q]).start()

                cross(d, q).start()

                @pl.when(q == 0)
                def _():
                    tags(d, d).wait_recv()
                    wave(d, d).wait_recv()
                    for o in range(1, mpos):
                        wave_share(d, o).start()
                    for o in range(1, mpos):
                        wave_shared(d, o).wait_recv()
                    wave_cross(d, c).start()

    def finish(t, q):
        for step in (1, -1):
            d = me - step * t

            @pl.when(jnp.logical_and(d >= 0, d < n))
            def _():
                @pl.when(q == 0)
                def _():
                    wave_cross(d, other).wait_recv()

                cross(d, q).wait_recv()
                compute(d, q)

    def turn(u, carry):
        @pl.when(u < (n - 1) * nw)
        def _():
            arrive(u // nw + 1, lax.rem(u, nw))

        @pl.when(u > 0)
        def _():
            finish((u - 1) // nw + 1, lax.rem(u + nw - 1, nw))

        return carry

    lax.fori_loop(0, (n - 1) * nw + 1, turn, 0)

    for q in range(nw):

        @pl.when(me + 1 < n)
        def _():
            hop(me, q, 1, ls_own.at[0, q]).wait_send()

        @pl.when(me > 0)
        def _():
            hop(me, q, -1, ls_own.at[1, q]).wait_send()

    def drain(d, carry):
        wave_cross(d, c).wait_send()
        for o in range(1, mpos):
            partial_to(d, o).wait()

        @pl.when(d != me)
        def _():
            wave(d, me).wait_send()
            for o in range(1, mpos):
                wave_share(d, o).wait_send()
            tags(d, me).wait_send()
            for q in range(nw):
                cross(d, q).wait_send()

        @pl.when(jnp.logical_and(d < me, me + 1 < n))
        def _():
            for q in range(nw):
                hop(d, q, 1, ls.at[d, q]).wait_send()

        @pl.when(jnp.logical_and(d > me, me > 0))
        def _():
            for q in range(nw):
                hop(d, q, -1, ls.at[d, q]).wait_send()

        return carry

    lax.fori_loop(0, n, drain, 0)

    def emit(i, carry):
        r = recv_ref[0, i]
        d, k = r // per, lax.rem(r, per)
        value = total[d, k, own, :]
        for o in range(1, mpos):
            value = value + mbuf[o - 1, d, k].astype(F32)
        out_ref[i] = value.astype(BF)
        return carry

    lax.fori_loop(0, n * per, emit, 0)


def local(
    n,
    mpos,
    wavefunction,
    left_env,
    right_env,
    send_order,
    recv_order,
    pair_left,
    pair_right,
    left_size,
    right_size,
    mpo_pattern,
):
    pairs, width, half = wavefunction.shape
    per = pairs // n
    lefts, nw = left_env.shape[:2]
    vmem = pl.BlockSpec(memory_space=pltpu.VMEM)
    dma = pltpu.SemaphoreType.DMA
    others = max(mpos - 1, 1)
    return pl.pallas_call(
        functools.partial(kernel, n, mpos),
        out_shape=jax.ShapeDtypeStruct((pairs, width // mpos, half), BF),
        in_specs=[pl.BlockSpec(memory_space=pltpu.HBM)] * 10,
        out_specs=vmem,
        scratch_shapes=[
            pltpu.VMEM(wavefunction.shape, BF),
            pltpu.VMEM(left_env.shape, BF),
            pltpu.VMEM(right_env.shape, BF),
            dma((3,)),
            pltpu.SMEM(send_order.shape, jnp.int32),
            pltpu.SMEM(recv_order.shape, jnp.int32),
            pltpu.SMEM(pair_left.shape, jnp.int32),
            pltpu.SMEM(pair_right.shape, jnp.int32),
            pltpu.SMEM(left_size.shape, jnp.int32),
            pltpu.SMEM(right_size.shape, jnp.int32),
            pltpu.SMEM(mpo_pattern.shape, jnp.int32),
            pltpu.SMEM((pairs,), jnp.int32),
            dma((7,)),
            pltpu.VMEM((n, nw, lefts, width, width), BF),
            pltpu.VMEM(right_env.shape, BF),
            pltpu.VMEM((n, per, width, half), BF),
            pltpu.VMEM((n, per, lefts, 16, 128), BF),
            pltpu.VMEM((n, 2, per, width, half), BF),
            pltpu.VMEM((n, per, lefts, 16, 128), BF),
            pltpu.VMEM((n, per, width, half), F32),
            pltpu.VMEM((n, per, width, half), BF),
            pltpu.VMEM((others, n, per, width // mpos, half), BF),
            dma((2, nw)),
            dma((n, nw)),
            dma((n, nw)),
            dma((n, nw)),
            dma((n, nw)),
            dma((n,)),
            dma((n,)),
            dma((n, others)),
            dma((n, others)),
            dma((n,)),
            dma((n,)),
            dma((n,)),
            dma((n,)),
            dma((n, others)),
            dma((n, others)),
        ],
        compiler_params=pltpu.CompilerParams(
            collective_id=0, has_side_effects=True, vmem_limit_bytes=64 * 1024 * 1024
        ),
        cost_estimate=pl.CostEstimate(
            flops=6 * pairs * nw * width * width * half,
            bytes_accessed=8 * pairs * width * half,
            transcendentals=0,
        ),
        name="apply_blocks",
    )(
        send_order,
        recv_order,
        pair_left,
        pair_right,
        left_size,
        right_size,
        mpo_pattern,
        wavefunction,
        left_env,
        right_env,
    )


def solution(mesh):
    placed = (
        P(("runs", "sec"), None, "rep"),
        P(("runs", "sec"), "mpo", None, None),
        P(("runs", "sec"), "mpo", None, "rep"),
        P("sec", None),
        P("sec", None),
        P("sec", None),
        P("sec", None),
        P("sec"),
        P("sec"),
        P("sec", "mpo"),
    )
    return jax.shard_map(
        functools.partial(local, mesh.shape["sec"], mesh.shape["mpo"]),
        mesh=mesh,
        in_specs=placed,
        out_specs=P(("runs", "sec"), "mpo", "rep"),
        check_vma=False,
    )
```

```python
import functools

import jax
import jax.numpy as jnp
from jax import lax
from jax.experimental import pallas as pl
from jax.experimental.pallas import tpu as pltpu
from jax.sharding import PartitionSpec as P

BF = jnp.bfloat16
F32 = jnp.float32
MESH = pl.DeviceIdType.MESH


def kernel(
    n,
    mpos,
    send_hbm,
    recv_hbm,
    pair_hbm,
    pair_right_hbm,
    lsize_hbm,
    rsize_hbm,
    pattern_hbm,
    wf_hbm,
    left_hbm,
    right_hbm,
    out_ref,
    wf_ref,
    left_ref,
    right_ref,
    load,
    send_ref,
    recv_ref,
    pair_ref,
    pair_right_ref,
    lsize_ref,
    rsize_ref,
    pattern_ref,
    right_of_ref,
    load_small,
    lbuf,
    rbuf,
    stage,
    tagstage,
    wbuf,
    tagbuf,
    total,
    rounded,
    mbuf,
    ls_own,
    ls,
    lr,
    cs,
    cr,
    ws,
    wr,
    xs,
    xr,
    vs,
    vr,
    ts,
    tr,
    ms,
    mr,
):
    me = lax.axis_index("sec")
    m = lax.axis_index("mpo")
    c = lax.axis_index("rep")
    other = 1 - c
    lefts, nw, width = left_ref.shape[:3]
    rights = right_ref.shape[0]
    half = wf_ref.shape[2]
    per = wf_ref.shape[0] // n
    part = width // 2
    mrows = width // mpos

    load_left = pltpu.make_async_copy(left_hbm, left_ref, load.at[0])
    load_wf = pltpu.make_async_copy(wf_hbm, wf_ref, load.at[1])
    load_right = pltpu.make_async_copy(right_hbm, right_ref, load.at[2])
    smalls = (
        (lsize_hbm, lsize_ref),
        (pattern_hbm, pattern_ref),
        (send_hbm, send_ref),
        (pair_hbm, pair_ref),
        (recv_hbm, recv_ref),
        (pair_right_hbm, pair_right_ref),
        (rsize_hbm, rsize_ref),
    )
    small = [pltpu.make_async_copy(a, b, load_small.at[i]) for i, (a, b) in enumerate(smalls)]
    for copy in small:
        copy.start()
    load_left.start()
    load_wf.start()
    load_right.start()
    barrier = pltpu.get_barrier_semaphore()
    for t in range(1, n):
        pl.semaphore_signal(
            barrier, inc=1, device_id={"sec": lax.rem(me + t, n)}, device_id_type=MESH
        )
    for t in range(1, mpos):
        pl.semaphore_signal(
            barrier, inc=1, device_id={"mpo": lax.rem(m + t, mpos)}, device_id_type=MESH
        )
    pl.semaphore_signal(barrier, inc=1, device_id={"rep": other}, device_id_type=MESH)

    row = lax.broadcasted_iota(jnp.int32, (width, width), 0)
    hrow = lax.broadcasted_iota(jnp.int32, (width, half), 0)
    hcol = lax.broadcasted_iota(jnp.int32, (width, half), 1) + c * half

    def my_rows(d, q):
        return lbuf.at[d, q, :, pl.ds(pl.multiple_of(c * part, part), part), :]

    def hop(d, q, step, sem):
        return pltpu.make_async_remote_copy(
            src_ref=my_rows(d, q),
            dst_ref=my_rows(d, q),
            send_sem=sem,
            recv_sem=lr.at[d, q],
            device_id={"sec": me + step},
            device_id_type=MESH,
        )

    def cross(d, q):
        return pltpu.make_async_remote_copy(
            src_ref=my_rows(d, q),
            dst_ref=my_rows(d, q),
            send_sem=cs.at[d, q],
            recv_sem=cr.at[d, q],
            device_id={"rep": other},
            device_id_type=MESH,
        )

    own = pl.ds(pl.multiple_of(m * mrows, mrows), mrows)

    def wave(e, slot):
        return pltpu.make_async_remote_copy(
            src_ref=stage.at[e, :, own, :],
            dst_ref=wbuf.at[slot, c, :, own, :],
            send_sem=ws.at[e],
            recv_sem=wr.at[slot],
            device_id={"sec": e},
            device_id_type=MESH,
        )

    def wave_share(d, o):
        return pltpu.make_async_remote_copy(
            src_ref=wbuf.at[d, c, :, own, :],
            dst_ref=wbuf.at[d, c, :, own, :],
            send_sem=xs.at[d, o - 1],
            recv_sem=xr.at[d, o - 1],
            device_id={"mpo": lax.rem(m + o, mpos)},
            device_id_type=MESH,
        )

    def wave_shared(d, o):
        source = lax.rem(m + mpos - o, mpos)
        rows = pl.ds(pl.multiple_of(source * mrows, mrows), mrows)
        return pltpu.make_async_remote_copy(
            src_ref=wbuf.at[d, c, :, rows, :],
            dst_ref=wbuf.at[d, c, :, rows, :],
            send_sem=xs.at[d, o - 1],
            recv_sem=xr.at[d, o - 1],
            device_id={"mpo": source},
            device_id_type=MESH,
        )

    def wave_cross(d, side):
        return pltpu.make_async_remote_copy(
            src_ref=wbuf.at[d, side],
            dst_ref=wbuf.at[d, side],
            send_sem=vs.at[d],
            recv_sem=vr.at[d],
            device_id={"rep": other},
            device_id_type=MESH,
        )

    def tags(e, slot):
        return pltpu.make_async_remote_copy(
            src_ref=tagstage.at[e],
            dst_ref=tagbuf.at[slot],
            send_sem=ts.at[e],
            recv_sem=tr.at[slot],
            device_id={"sec": e},
            device_id_type=MESH,
        )

    def partial_to(d, o):
        target = lax.rem(m + o, mpos)
        rows = pl.ds(pl.multiple_of(target * mrows, mrows), mrows)
        return pltpu.make_async_remote_copy(
            src_ref=rounded.at[d, :, rows, :],
            dst_ref=mbuf.at[o - 1, d],
            send_sem=ms.at[d, o - 1],
            recv_sem=mr.at[d, o - 1],
            device_id={"mpo": target},
            device_id_type=MESH,
        )

    for copy in small:
        copy.wait()
    keeps = [jnp.where(row < lsize_ref[l], 1.0, 0.0) for l in range(lefts)]
    pl.semaphore_wait(barrier, n + mpos - 1)
    load_wf.wait()

    def fill(e, carry):
        for k in range(per):
            block = send_ref[0, e * per + k]
            left = pair_ref[0, block]
            keep = jnp.where(hrow < lsize_ref[left], 1.0, 0.0).astype(BF)
            stage[e, k] = wf_ref[block] * keep
            for l in range(lefts):
                flag = jnp.where(left == l, 1.0, 0.0)
                tagstage[e, k, l] = jnp.full((16, 128), flag, F32).astype(BF)

        @pl.when(e != me)
        def _():
            tags(e, me).start()
            wave(e, me).start()

        return carry

    lax.fori_loop(0, n, fill, 0)

    load_left.wait()
    for q in range(nw):
        for l in range(lefts):
            scale = (keeps[l] * pattern_ref[l, q].astype(F32)).astype(BF)
            lbuf[me, q, l] = left_ref[l, q] * scale

        @pl.when(me + 1 < n)
        def _():
            hop(me, q, 1, ls_own.at[0, q]).start()

        @pl.when(me > 0)
        def _():
            hop(me, q, -1, ls_own.at[1, q]).start()

    wbuf[me, c] = stage[me]
    tagbuf[me] = tagstage[me]
    wave_cross(me, c).start()

    def invert(r, carry):
        b = jnp.int32(0)
        for i in range(n * per):
            b = jnp.where(recv_ref[0, i] == r, pair_right_ref[0, i], b)
        right_of_ref[r] = b
        return carry

    lax.fori_loop(0, n * per, invert, 0)

    load_right.wait()
    for b in range(rights):
        size = rsize_ref[b]
        keep = jnp.where(jnp.logical_and(hrow < size, hcol < size), 1.0, 0.0).astype(BF)
        for w in range(nw):
            rbuf[b, w] = right_ref[b, w] * keep

    def compute(d, q):
        for k in range(per):
            x = jnp.concatenate([wbuf[d, 0, k], wbuf[d, 1, k]], axis=1)
            b = right_of_ref[d * per + k]
            env = None
            for l in range(lefts):
                flag = tagbuf[d, k, l]
                flag = jnp.concatenate([flag] * (width // 128), axis=1)
                flag = jnp.concatenate([flag] * (width // 16), axis=0)
                term = lbuf[d, q, l] * flag
                env = term if env is None else env + term
            y = jnp.dot(env, x, preferred_element_type=F32).astype(BF)
            total[d, k] += jnp.dot(y, rbuf[b, q], preferred_element_type=F32)

        @pl.when(q == nw - 1)
        def _():
            for k in range(per):
                rounded[d, k] = total[d, k].astype(BF)
            for o in range(1, mpos):
                partial_to(d, o).start()

    def clear(d, carry):
        for k in range(per):
            total[d, k] = jnp.zeros((width, half), F32)
        return carry

    lax.fori_loop(0, n, clear, 0)

    wave_cross(me, other).wait_recv()

    def first(q, carry):
        compute(me, q)
        return carry

    lax.fori_loop(0, nw, first, 0)

    def arrive(t, q):
        for step in (1, -1):
            d = me - step * t

            @pl.when(jnp.logical_and(d >= 0, d < n))
            def _():
                hop(d, q, -step, ls.at[d, q]).wait_recv()
                nxt = me + step

                @pl.when(jnp.logical_and(nxt >= 0, nxt < n))
                def _():
                    hop(d, q, step, ls.at[d, q]).start()

                cross(d, q).start()

                @pl.when(q == 0)
                def _():
                    tags(d, d).wait_recv()
                    wave(d, d).wait_recv()
                    for o in range(1, mpos):
                        wave_share(d, o).start()
                    for o in range(1, mpos):
                        wave_shared(d, o).wait_recv()
                    wave_cross(d, c).start()

    def finish(t, q):
        for step in (1, -1):
            d = me - step * t

            @pl.when(jnp.logical_and(d >= 0, d < n))
            def _():
                @pl.when(q == 0)
                def _():
                    wave_cross(d, other).wait_recv()

                cross(d, q).wait_recv()
                compute(d, q)

    def turn(u, carry):
        @pl.when(u < (n - 1) * nw)
        def _():
            arrive(u // nw + 1, lax.rem(u, nw))

        @pl.when(u > 0)
        def _():
            finish((u - 1) // nw + 1, lax.rem(u + nw - 1, nw))

        return carry

    lax.fori_loop(0, (n - 1) * nw + 1, turn, 0)

    for q in range(nw):

        @pl.when(me + 1 < n)
        def _():
            hop(me, q, 1, ls_own.at[0, q]).wait_send()

        @pl.when(me > 0)
        def _():
            hop(me, q, -1, ls_own.at[1, q]).wait_send()

    def drain(d, carry):
        wave_cross(d, c).wait_send()
        for o in range(1, mpos):
            partial_to(d, o).wait()

        @pl.when(d != me)
        def _():
            wave(d, me).wait_send()
            for o in range(1, mpos):
                wave_share(d, o).wait_send()
            tags(d, me).wait_send()
            for q in range(nw):
                cross(d, q).wait_send()

        @pl.when(jnp.logical_and(d < me, me + 1 < n))
        def _():
            for q in range(nw):
                hop(d, q, 1, ls.at[d, q]).wait_send()

        @pl.when(jnp.logical_and(d > me, me > 0))
        def _():
            for q in range(nw):
                hop(d, q, -1, ls.at[d, q]).wait_send()

        return carry

    lax.fori_loop(0, n, drain, 0)

    def emit(i, carry):
        r = recv_ref[0, i]
        d, k = r // per, lax.rem(r, per)
        value = total[d, k, own, :]
        for o in range(1, mpos):
            value = value + mbuf[o - 1, d, k].astype(F32)
        out_ref[i] = value.astype(BF)
        return carry

    lax.fori_loop(0, n * per, emit, 0)


def local(
    n,
    mpos,
    wavefunction,
    left_env,
    right_env,
    send_order,
    recv_order,
    pair_left,
    pair_right,
    left_size,
    right_size,
    mpo_pattern,
):
    pairs, width, half = wavefunction.shape
    per = pairs // n
    lefts, nw = left_env.shape[:2]
    vmem = pl.BlockSpec(memory_space=pltpu.VMEM)
    dma = pltpu.SemaphoreType.DMA
    others = max(mpos - 1, 1)
    return pl.pallas_call(
        functools.partial(kernel, n, mpos),
        out_shape=jax.ShapeDtypeStruct((pairs, width // mpos, half), BF),
        in_specs=[pl.BlockSpec(memory_space=pltpu.HBM)] * 10,
        out_specs=vmem,
        scratch_shapes=[
            pltpu.VMEM(wavefunction.shape, BF),
            pltpu.VMEM(left_env.shape, BF),
            pltpu.VMEM(right_env.shape, BF),
            dma((3,)),
            pltpu.SMEM(send_order.shape, jnp.int32),
            pltpu.SMEM(recv_order.shape, jnp.int32),
            pltpu.SMEM(pair_left.shape, jnp.int32),
            pltpu.SMEM(pair_right.shape, jnp.int32),
            pltpu.SMEM(left_size.shape, jnp.int32),
            pltpu.SMEM(right_size.shape, jnp.int32),
            pltpu.SMEM(mpo_pattern.shape, jnp.int32),
            pltpu.SMEM((pairs,), jnp.int32),
            dma((7,)),
            pltpu.VMEM((n, nw, lefts, width, width), BF),
            pltpu.VMEM(right_env.shape, BF),
            pltpu.VMEM((n, per, width, half), BF),
            pltpu.VMEM((n, per, lefts, 16, 128), BF),
            pltpu.VMEM((n, 2, per, width, half), BF),
            pltpu.VMEM((n, per, lefts, 16, 128), BF),
            pltpu.VMEM((n, per, width, half), F32),
            pltpu.VMEM((n, per, width, half), BF),
            pltpu.VMEM((others, n, per, width // mpos, half), BF),
            dma((2, nw)),
            dma((n, nw)),
            dma((n, nw)),
            dma((n, nw)),
            dma((n, nw)),
            dma((n,)),
            dma((n,)),
            dma((n, others)),
            dma((n, others)),
            dma((n,)),
            dma((n,)),
            dma((n,)),
            dma((n,)),
            dma((n, others)),
            dma((n, others)),
        ],
        compiler_params=pltpu.CompilerParams(
            collective_id=0, has_side_effects=True, vmem_limit_bytes=64 * 1024 * 1024
        ),
        cost_estimate=pl.CostEstimate(
            flops=6 * pairs * nw * width * width * half,
            bytes_accessed=8 * pairs * width * half,
            transcendentals=0,
        ),
        name="apply_blocks",
    )(
        send_order,
        recv_order,
        pair_left,
        pair_right,
        left_size,
        right_size,
        mpo_pattern,
        wavefunction,
        left_env,
        right_env,
    )


def solution(mesh):
    placed = (
        P(("runs", "sec"), None, "rep"),
        P(("runs", "sec"), "mpo", None, None),
        P(("runs", "sec"), "mpo", None, "rep"),
        P("sec", None),
        P("sec", None),
        P("sec", None),
        P("sec", None),
        P("sec"),
        P("sec"),
        P("sec", "mpo"),
    )
    return jax.shard_map(
        functools.partial(local, mesh.shape["sec"], mesh.shape["mpo"]),
        mesh=mesh,
        in_specs=placed,
        out_specs=P(("runs", "sec"), "mpo", "rep"),
        check_vma=False,
    )
```
